32 devices in a mesh: cases: 2 (over y), gx: 4 (over z), gy: 2 (over x), af: 2 (over core).
Axes of the slice: x: 2, y: 2, z: 4, core: 2. Of those that a mesh axis runs over, the one named last changes fastest.
Arguments:
- state_zero: float32 [5, 4, 64, 256], P(None, 'af', ('cases', 'gx'), 'gy'), parts along dimension 2, may hold values from -4 to 17, as said below
- state_one: float32 [5, 4, 64, 256], P(None, 'af', ('cases', 'gx'), 'gy'), parts along dimension 2, may hold values from -4 to 17, as said below
- cotangent: float32 [5, 4, 64, 256], P(None, 'af', ('cases', 'gx'), 'gy'), parts along dimension 2, may hold values from -45 to 45
- weight_in: float32 [64, 5], replicated, may hold values from -2.5 to 2.5
- bias_in: float32 [64], replicated, may hold values from -3 to 3
- weight_out: float32 [5, 64], replicated, may hold values from -0.75 to 0.75
- bias_out: float32 [5], replicated, may hold values from -3 to 3
Outputs:
- grad_state: float32 [5, 4, 64, 256], P(None, 'af', ('cases', 'gx'), 'gy'), parts along dimension 2
- grad_weight_in: float32 [128, 5], P('cases'), parts along dimension 0
- grad_bias_in: float32 [128], P('cases'), parts along dimension 0
- grad_weight_out: float32 [10, 64], P('cases'), parts along dimension 0
- grad_bias_out: float32 [10], P('cases'), parts along dimension 0
The draws below stay inside these ranges and needn't reach their ends.
There are 2 independent parts, one for each index of `cases`. The reference program is written for one: setup_inputs(seed, part) draws one part's arguments, and reference() takes and returns one part's arrays. A program takes and returns all parts, laid end to end along the dimension named above; an argument that names none is the same for every part. Nothing has to cross between parts.
Inputs may be any that keep to these rules, and one draw needn't show every extreme that they name: `state_zero`: field 0 (density) lies in 0.5 to 2, velocities (fields 1 to 3 over field 0) in -2 to 2 and pressure in 0.5 to 2 at every cell. `state_one`: field 0 (density) lies in 0.5 to 2, velocities (fields 1 to 3 over field 0) in -2 to 2 and pressure in 0.5 to 2 at every cell.
All inputs are finite; a program needn't handle non-finite values.
Results may differ from the reference program's by a relative error of at most 0.00016.
Values sent between devices are 32-bit elements; how exact they have to be, the bound alone decides.
A program may use at most 64 MiB of HBM per device.

```python
import math
import jax
import jax.numpy as jnp
from jax import lax

NZ = 4
H = 64
NX = 32
NY = 256


def draw_state_zero(key, part):
    key = jax.random.fold_in(key, 11)
    keys = jax.random.split(key, 3)
    shape = (NZ, NX, NY)
    density = jnp.exp(jax.random.uniform(keys[0], shape, jnp.float32, math.log(0.5), math.log(2.0)))
    velocity = jnp.clip(0.5 * jax.random.normal(keys[1], (3,) + shape, jnp.float32), -2.0, 2.0)
    pressure = jnp.exp(jax.random.uniform(keys[2], shape, jnp.float32, math.log(0.5), math.log(2.0)))
    energy = pressure / 0.4 + 0.5 * density * jnp.sum(velocity * velocity, axis=0)
    return jnp.stack([density, density * velocity[0], density * velocity[1], density * velocity[2], energy]).astype(jnp.float32)


def draw_state_one(key, part):
    key = jax.random.fold_in(key, 23)
    keys = jax.random.split(key, 3)
    shape = (NZ, NX, NY)
    density = jnp.exp(jax.random.uniform(keys[0], shape, jnp.float32, math.log(0.5), math.log(2.0)))
    velocity = jnp.clip(0.5 * jax.random.normal(keys[1], (3,) + shape, jnp.float32), -2.0, 2.0)
    pressure = jnp.exp(jax.random.uniform(keys[2], shape, jnp.float32, math.log(0.5), math.log(2.0)))
    energy = pressure / 0.4 + 0.5 * density * jnp.sum(velocity * velocity, axis=0)
    return jnp.stack([density, density * velocity[0], density * velocity[1], density * velocity[2], energy]).astype(jnp.float32)


def draw_cotangent(key, part):
    key = jax.random.fold_in(key, 37)
    keys = jax.random.split(key, 2)
    shape = (5, NZ, NX, NY)
    position = jnp.arange(NX, dtype=jnp.float32).reshape((1, 1, NX, 1))
    rising = 1.0 + 2.0 * position / max(NX - 1, 1)
    rough = jnp.exp(math.log(10.0) * jax.random.uniform(keys[0], shape, jnp.float32)) / 3.0
    base = jnp.clip(jax.random.normal(keys[1], shape, jnp.float32) + 0.3, -4.0, 4.0)
    return (rising * rough * base).astype(jnp.float32)


def normal_values(stream_key, extent, deviation, limit, held_as=jnp.bfloat16):
    values = deviation * jax.random.normal(stream_key, extent, jnp.float32)
    return jnp.clip(values, min=-limit, max=limit).astype(held_as)


def setup_inputs(seed: int = 0, part: int = 0) -> dict:
    seeds = jax.random.split(jax.random.key(seed), 8)
    part_splits = jax.random.split(jax.random.fold_in(seeds[7], part), 8)
    state_zero = draw_state_zero(jax.random.fold_in(jax.random.fold_in(seeds[7], part), 71), part)
    state_one = draw_state_one(jax.random.fold_in(jax.random.fold_in(seeds[7], part), 71), part)
    cotangent = draw_cotangent(jax.random.fold_in(jax.random.fold_in(seeds[7], part), 71), part)
    weight_in = normal_values(seeds[3], (H, 5), 5 ** -0.5, 2.5, jnp.float32)
    bias_in = normal_values(seeds[4], (H,), 0.5, 3.0, jnp.float32)
    weight_out = normal_values(seeds[5], (5, H), H ** -0.5, 0.75, jnp.float32)
    bias_out = normal_values(seeds[6], (5,), 0.5, 3.0, jnp.float32)
    return {"state_zero": state_zero, "state_one": state_one, "cotangent": cotangent, "weight_in": weight_in, "bias_in": bias_in, "weight_out": weight_out, "bias_out": bias_out}


GAMMA = 1.4
TIME_STEP = 0.1
VISCOSITY = 0.2
WENO_EPS = 1e-06

def pressure_of(fields):
    kinetic = 0.5 * (fields[1] * fields[1] + fields[2] * fields[2] + fields[3] * fields[3]) / fields[0]
    return (GAMMA - 1.0) * (fields[4] - kinetic)

def max_speed(fields):
    density = fields[0]
    sound = jnp.sqrt(GAMMA * pressure_of(fields) / density)
    along = jnp.maximum(jnp.abs(fields[1] / density), jnp.abs(fields[2] / density))
    return jnp.max(along + sound)

def face_flux(fields, normal_index):
    pressure = pressure_of(fields)
    velocity = fields[normal_index + 1] / fields[0]
    parts = [fields[0] * velocity, fields[1] * velocity, fields[2] * velocity, fields[3] * velocity, (fields[4] + pressure) * velocity]
    parts[normal_index + 1] = parts[normal_index + 1] + pressure
    return jnp.stack(parts)

def weno_face(cell_a, cell_b, cell_c, cell_d, cell_e):
    smooth_a = 13.0 / 12.0 * (cell_a - 2.0 * cell_b + cell_c) ** 2 + 0.25 * (cell_a - 4.0 * cell_b + 3.0 * cell_c) ** 2
    smooth_b = 13.0 / 12.0 * (cell_b - 2.0 * cell_c + cell_d) ** 2 + 0.25 * (cell_b - cell_d) ** 2
    smooth_c = 13.0 / 12.0 * (cell_c - 2.0 * cell_d + cell_e) ** 2 + 0.25 * (3.0 * cell_c - 4.0 * cell_d + cell_e) ** 2
    weight_a = 0.1 / (WENO_EPS + smooth_a) ** 2
    weight_b = 0.6 / (WENO_EPS + smooth_b) ** 2
    weight_c = 0.3 / (WENO_EPS + smooth_c) ** 2
    guess_a = (2.0 * cell_a - 7.0 * cell_b + 11.0 * cell_c) / 6.0
    guess_b = (-cell_b + 5.0 * cell_c + 2.0 * cell_d) / 6.0
    guess_c = (2.0 * cell_c + 5.0 * cell_d - cell_e) / 6.0
    return (weight_a * guess_a + weight_b * guess_b + weight_c * guess_c) / (weight_a + weight_b + weight_c)

def divergence(fields, dim_index, normal_index, wave_speed):
    flux_all = face_flux(fields, normal_index)
    upwind = 0.5 * (flux_all + wave_speed * fields)
    downwind = 0.5 * (flux_all - wave_speed * fields)
    faces = fields.shape[dim_index] - 5

    def cell_run(source, start):
        return lax.slice_in_dim(source, start, start + faces, axis=dim_index)
    face_sum = weno_face(cell_run(upwind, 0), cell_run(upwind, 1), cell_run(upwind, 2), cell_run(upwind, 3), cell_run(upwind, 4))
    face_sum = face_sum + weno_face(cell_run(downwind, 5), cell_run(downwind, 4), cell_run(downwind, 3), cell_run(downwind, 2), cell_run(downwind, 1))
    upper = lax.slice_in_dim(face_sum, 1, faces, axis=dim_index)
    lower = lax.slice_in_dim(face_sum, 0, faces - 1, axis=dim_index)
    return lower - upper

def flux_rhs(fields, wave_speed):
    final_dim = fields.ndim - 1
    along_x = divergence(fields, final_dim - 1, 0, wave_speed)[..., 3:-3]
    along_y = divergence(fields, final_dim, 1, wave_speed)[..., 3:-3, :]
    center = fields[..., 3:-3, 3:-3]
    laplace = fields[..., 4:-2, 3:-3] + fields[..., 2:-4, 3:-3] + fields[..., 3:-3, 4:-2] + fields[..., 3:-3, 2:-4] - 4.0 * center
    momentum_mask = jnp.array([0.0, 1.0, 1.0, 1.0, 1.0], jnp.float32).reshape((5,) + (1,) * (fields.ndim - 1))
    return along_x + along_y + VISCOSITY * momentum_mask * laplace

def closure(fields, weight_in, bias_in, weight_out, bias_out):
    shape_tail = (1,) * (fields.ndim - 1)
    hidden = jnp.tanh(jnp.einsum('hf,f...->h...', weight_in, fields, precision=lax.Precision.HIGHEST) + bias_in.reshape((-1,) + shape_tail))
    return fields[0] * (jnp.einsum('fh,h...->f...', weight_out, hidden, precision=lax.Precision.HIGHEST) + bias_out.reshape((-1,) + shape_tail))

def section_adjoint(state, cotangent, wave_speed, weight_in, bias_in, weight_out, bias_out):

    def per_plane(pair):
        plane, cot_plane = pair

        def flux_part(source):
            return flux_rhs(jnp.pad(source, ((0, 0), (3, 3), (3, 3)), mode='wrap'), wave_speed)
        _, flux_back = jax.vjp(flux_part, plane)
        _, closure_back = jax.vjp(closure, plane, weight_in, bias_in, weight_out, bias_out)
        pieces = closure_back(cot_plane)
        return (flux_back(cot_plane)[0] + pieces[0], pieces[1:])
    moved, grads = lax.map(per_plane, (jnp.moveaxis(state, 1, 0), jnp.moveaxis(cotangent, 1, 0)))
    return (jnp.moveaxis(moved, 0, 1), jax.tree.map(lambda stacked: lax.optimization_barrier(jnp.sum(stacked, axis=0)), grads))

def reference(state_zero, state_one, cotangent, weight_in, bias_in, weight_out, bias_out):
    speed_zero = max_speed(state_zero)
    speed_one = max_speed(state_one)
    flux_one, grads_one = section_adjoint(state_one, cotangent, speed_one, weight_in, bias_in, weight_out, bias_out)
    grad_middle = 0.25 * cotangent + 0.25 * TIME_STEP * flux_one
    flux_zero, grads_zero = section_adjoint(state_zero, grad_middle, speed_zero, weight_in, bias_in, weight_out, bias_out)
    grad_state = 0.75 * cotangent + grad_middle + TIME_STEP * flux_zero
    scale = 1.0 / (NX * NY * NZ)
    totals = jax.tree.map(lambda first, second: (0.25 * TIME_STEP * first + TIME_STEP * second) * scale, grads_one, grads_zero)
    return (grad_state, totals[0], totals[1], totals[2], totals[3])
```

```python
import functools

import jax
import jax.numpy as jnp
from jax import lax
from jax.experimental import pallas as pl
from jax.experimental.pallas import tpu as pltpu
from jax.sharding import PartitionSpec as P

MESH = pl.DeviceIdType.MESH
GAMMA = 1.4
TIME_STEP = 0.1
VISCOSITY = 0.2
WENO_EPS = 1e-06
F32 = jnp.float32
BF16 = jnp.bfloat16


def shifted(x, by, axis):
    return pltpu.roll(x, (-by) % x.shape[axis], axis)


def high_low(x):
    high = x.astype(BF16).astype(F32)
    return high, x - high


def weno_grads(d0, d1, d2, d3, w):
    a0 = 8.0 * d0 - 11.0 * d1
    a1 = 20.0 * d1 - 11.0 * d0
    b0 = 8.0 * d1 - 5.0 * d2
    b1 = 8.0 * d2 - 5.0 * d1
    c0 = 20.0 * d2 - 11.0 * d3
    c1 = 8.0 * d3 - 11.0 * d2
    eps = 6.0 * WENO_EPS
    ra = 1.0 / (eps + d0 * a0 + d1 * a1)
    rb = 1.0 / (eps + d1 * b0 + d2 * b1)
    rc = 1.0 / (eps + d2 * c0 + d3 * c1)
    wa = ra * ra
    wb = 6.0 * (rb * rb)
    wc = 3.0 * (rc * rc)
    ga = 5.0 * d1 - 2.0 * d0
    gb = d1 + 2.0 * d2
    gc = 4.0 * d2 - d3
    inv = 1.0 / (wa + wb + wc)
    mean = (wa * ga + wb * gb + wc * gc) * inv
    scale = w * inv
    ka = wa * scale
    kb = wb * scale
    kc = wc * scale
    ma = 4.0 * ka * ra * (mean - ga)
    mb = 4.0 * kb * rb * (mean - gb)
    mc = 4.0 * kc * rc * (mean - gc)
    return (
        ma * a0 - 2.0 * ka,
        ma * a1 + 5.0 * ka + mb * b0 + kb,
        mb * b1 + 2.0 * kb + mc * c0 + 4.0 * kc,
        mc * c1 - kc,
    )


def line_adjoint(up, down, v, axis, own):
    sh = functools.partial(shifted, axis=axis)
    w = sh(v, 1) - v
    w6 = w * (1.0 / 6.0)
    d = sh(up, 1) - up
    g = weno_grads(sh(d, -2), sh(d, -1), d, sh(d, 1), w6)
    gp = sh(g[0], 2) + sh(g[1], 1) + g[2] + sh(g[3], -1)
    d = down - sh(down, 1)
    g = weno_grads(sh(d, 2), sh(d, 1), d, sh(d, -1), w6)
    gm = sh(g[0], -2) + sh(g[1], -1) + g[2] + sh(g[3], 1)
    wb = sh(w, -1)
    t = gp - gm
    s = gp + gm
    total = w + wb + sh(t, -1) - t
    apart = w - wb + sh(s, -1) - s
    laplace = sh(v, 1) + sh(v, -1) - 2.0 * v
    return own(total), own(apart), own(laplace)


def flux_parts(q, k):
    inv = 1.0 / q[0]
    pressure = (GAMMA - 1.0) * (
        q[4] - 0.5 * (q[1] * q[1] + q[2] * q[2] + q[3] * q[3]) * inv
    )
    u = q[k + 1] * inv
    f = [q[k + 1], q[1] * u, q[2] * u, q[3] * u, (q[4] + pressure) * u]
    f[k + 1] = f[k + 1] + pressure
    return f


def kernel(
    sizes,
    s0_ref, s1_ref, ct_ref, win_ref, bin_ref, wout_ref, bout_ref,
    out_ref, gwin_ref, gbin_ref, gwout_ref, gbout_ref,
    q0p, q1p, ctp, gmp, cqp, wtile, w1, w2, w3, bcol,
    fxp, fxm, fyp, fym, vx, vy, gx_s, gy_s, gq_s,
    xs, xr, ys, yr, spd, prm,
    xsend, xrecv, ysend, yrecv, gsend, grecv, psend, precv,
):
    GX, GY, AF = sizes
    ix, iy, ia = lax.axis_index("gx"), lax.axis_index("gy"), lax.axis_index("af")
    ic = lax.axis_index("cases")
    joint = GX * GY * AF <= 16
    if joint:
        stages = [[(a, b, c) for a in range(GX) for b in range(GY) for c in range(AF)]]
    else:
        stages = [
            [(a, 0, 0) for a in range(GX)],
            [(0, b, 0) for b in range(GY)],
            [(0, 0, c) for c in range(AF)],
        ]

    def place(off):
        return (
            ic,
            lax.rem(ix + off[0], GX) if off[0] else ix,
            lax.rem(iy + off[1], GY) if off[1] else iy,
            lax.rem(ia + off[2], AF) if off[2] else ia,
        )

    barrier = pltpu.get_barrier_semaphore()
    greeted = 0
    for stage in stages:
        for off in stage[1:]:
            pl.semaphore_signal(barrier, inc=1, device_id=place(off), device_id_type=MESH)
            greeted += 1

    row = lax.broadcasted_iota(jnp.int32, (8, 128), 0)
    lane = lax.broadcasted_iota(jnp.int32, (8, 128), 1)
    upper = row < 4

    ones = jnp.ones((16, 128), F32)
    for ref, src in ((q0p, s0_ref), (q1p, s1_ref), (ctp, ct_ref)):
        ref[0:80, :] = src[...]
    for ref in (q0p, q1p):
        ref[80:96, :] = ones
        ref[96:128, :] = jnp.zeros((32, 128), F32)
    for ref in (ctp, gmp):
        ref[80:128, :] = jnp.zeros((48, 128), F32)

    def tile(ref, f, z):
        return ref[f * 16 + z * 8 : f * 16 + z * 8 + 8, :]

    def pack(ref, base, yslot):
        packed = jnp.zeros((8, 128), F32)
        for f in range(5):
            one, two = tile(ref, f, 0), pltpu.roll(tile(ref, f, 1), 4, 0)
            xs[0, base + f] = jnp.where(upper, one, two)
            xs[1, base + f] = jnp.where(upper, two, one)
            for z in range(2):
                t = f * 2 + z
                moved = pltpu.roll(tile(ref, f, z), (4 + 8 * t) % 128, 1)
                packed = jnp.where((lane >= 8 * t) & (lane < 8 * t + 8), moved, packed)
        ys[yslot] = packed

    def x_copies(base, count, sem):
        made = []
        for way in range(2):
            off = (GX - 1, 0, 0) if way == 0 else (1, 0, 0)
            made.append(
                pltpu.make_async_remote_copy(
                    src_ref=xs.at[way, pl.ds(base, count)],
                    dst_ref=xr.at[way, pl.ds(base, count)],
                    send_sem=xsend.at[way, sem],
                    recv_sem=xrecv.at[way, sem],
                    device_id=place(off),
                    device_id_type=MESH,
                )
            )
        return made

    def y_copies(base, count, sem):
        made = []
        for way in range(1 if GY == 2 else 2):
            off = (0, 1, 0) if way == 0 else (0, GY - 1, 0)
            made.append(
                pltpu.make_async_remote_copy(
                    src_ref=ys.at[pl.ds(base, count)],
                    dst_ref=yr.at[way, pl.ds(base, count)],
                    send_sem=ysend.at[way, sem],
                    recv_sem=yrecv.at[way, sem],
                    device_id=place(off),
                    device_id_type=MESH,
                )
            )
        return made

    def x_halo(base, f):
        ahead, behind = xr[0, base + f], xr[1, base + f]
        return (
            jnp.where(upper, ahead, behind),
            pltpu.roll(jnp.where(upper, behind, ahead), 4, 0),
        )

    def y_packed(slot):
        if GY == 2:
            return yr[0, slot]
        return jnp.where(lax.rem(lane, 8) < 4, yr[0, slot], yr[1, slot])

    def y_halo(packed, f, z):
        return pltpu.roll(packed, (-(4 + 8 * (f * 2 + z))) % 128, 1)

    pack(q1p, 0, 0)
    pack(ctp, 5, 1)
    pack(q0p, 10, 2)

    def top_speed(ref):
        best = None
        for z in range(2):
            q = [tile(ref, f, z) for f in range(5)]
            inv = 1.0 / q[0]
            pressure = (GAMMA - 1.0) * (
                q[4] - 0.5 * (q[1] * q[1] + q[2] * q[2] + q[3] * q[3]) * inv
            )
            sound = jnp.sqrt(GAMMA * pressure * inv)
            value = jnp.maximum(jnp.abs(q[1] * inv), jnp.abs(q[2] * inv)) + sound
            best = value if best is None else jnp.maximum(best, value)
        best = jnp.max(best, axis=0, keepdims=True)
        return jnp.broadcast_to(jnp.max(best, axis=1, keepdims=True), (1, 128))

    fastest = jnp.concatenate([top_speed(q0p), top_speed(q1p)], axis=1)

    wtile[...] = jnp.zeros_like(wtile)
    wtile[0:64, 0:5] = win_ref[...]
    wint = jnp.transpose(wtile[...])[0:8, :]
    wtile[0:8, :] = jnp.zeros((8, 128), F32)
    wtile[0:5, 0:64] = wout_ref[...]
    wout8 = wtile[0:8, :]
    wtile[0:8, :] = jnp.zeros((8, 128), F32)
    wtile[0:1, 0:64] = bin_ref[...]
    wtile[1:2, 0:5] = bout_ref[...]
    bin_row = wtile[0:1, :]
    bout_row = wtile[1:2, :]
    aug = jnp.where(row == 5, bin_row, wint)
    zero8 = jnp.zeros((8, 128), F32)
    ah, al = high_low(aug)
    oh, ol = high_low(wout8)
    fill = jnp.zeros((96, 128), F32)
    w1[...] = jnp.transpose(jnp.concatenate([ah, ah, al, zero8, fill], axis=0))[0:64, 0:32].astype(BF16)
    w2[...] = jnp.transpose(jnp.concatenate([oh, oh, ol, zero8, fill], axis=0))[0:64, 0:32].astype(BF16)
    ih, il = high_low(wint)
    lo_lane = lane < 64
    first = jnp.where(lo_lane, ih, pltpu.roll(ih, 64, 1))
    w3[:, 0:128] = jnp.concatenate([first, zero8], axis=0).astype(BF16)
    w3[:, 128:256] = jnp.concatenate([jnp.where(lo_lane, il, 0.0), zero8], axis=0).astype(BF16)
    bcol[...] = jnp.broadcast_to(
        jnp.sum(jnp.where(lane == row, jnp.broadcast_to(bout_row, (8, 128)), 0.0), axis=1, keepdims=True),
        (8, 128),
    )

    pl.semaphore_wait(barrier, greeted)

    a_copies = x_copies(0, 10, 0) + y_copies(0, 2, 0)
    b_copies = x_copies(10, 5, 1) + y_copies(2, 1, 1)
    c_copies = x_copies(15, 5, 2) + y_copies(3, 1, 2)

    def numbers(stage_index):
        base = sum(len(stages[s]) for s in range(stage_index))
        return [base + k for k in range(len(stages[stage_index]))]

    def my_rank(stage_index):
        if joint:
            return (ix * GY + iy) * AF + ia
        return (ix, iy, ia)[stage_index]

    def group_copies(buf, send, recv, stage_index):
        base = numbers(stage_index)[0]
        rank = base + my_rank(stage_index)
        made = []
        for k, off in enumerate(stages[stage_index]):
            if k == 0:
                continue
            made.append(
                pltpu.make_async_remote_copy(
                    src_ref=buf.at[rank],
                    dst_ref=buf.at[rank],
                    send_sem=send.at[base + k],
                    recv_sem=recv.at[base + k],
                    device_id=place(off),
                    device_id_type=MESH,
                )
            )
        return made

    started = []

    def start(copies):
        for c in copies:
            c.start()
            started.append(c)

    def begin_stage(buf, send, recv, s, value):
        buf[numbers(s)[0] + my_rank(s)] = value
        copies = group_copies(buf, send, recv, s)
        start(copies)
        return copies

    def end_stage(buf, s, copies, op):
        for c in copies:
            c.wait_recv()
        total = None
        for n in numbers(s):
            total = buf[n] if total is None else op(total, buf[n])
        return total

    spd_copies = begin_stage(spd, gsend, grecv, 0, fastest)
    start(a_copies)
    start(b_copies)

    def closure_back(qp, cp):
        acc = jnp.zeros((32, 256), F32)
        dsum = jnp.zeros((8, 256), F32)
        bb = jnp.concatenate([bcol[...], bcol[...]], axis=1)
        for chunk in range(8):
            r = 2 * chunk
            q8 = jnp.concatenate([qp[pl.ds(r, 8, stride=16), :], qp[pl.ds(r + 1, 8, stride=16), :]], axis=1)
            c8 = jnp.concatenate([cp[pl.ds(r, 8, stride=16), :], cp[pl.ds(r + 1, 8, stride=16), :]], axis=1)
            zero = jnp.zeros((8, 256), F32)
            qh, ql = high_low(q8)
            ch, cl = high_low(c8)
            pre = jnp.dot(w1[...], jnp.concatenate([qh, ql, qh, zero], axis=0).astype(BF16), preferred_element_type=F32)
            g = jnp.dot(w2[...], jnp.concatenate([ch, cl, ch, zero], axis=0).astype(BF16), preferred_element_type=F32)
            h = jnp.tanh(pre)
            t = g * (1.0 - h * h)
            hg = bb * c8
            prod = h * g
            for k in range(8):
                hg = hg + prod[8 * k : 8 * k + 8, :]
            hg = jnp.sum(hg, axis=0, keepdims=True)
            th, tl = high_low(t)
            hh, hl = high_low(h)
            thb, tlb = th.astype(BF16), tl.astype(BF16)
            hhb, hlb = hh.astype(BF16), hl.astype(BF16)
            stack = jnp.concatenate([thb, tlb, thb, jnp.zeros((64, 256), BF16)], axis=0)
            dq = jnp.dot(w3[...], stack, preferred_element_type=F32)[0:8, :]
            dens = q8[0:1, :]
            row2 = lax.broadcasted_iota(jnp.int32, (8, 256), 0)
            dq = dens * dq + jnp.where(row2 == 0, hg, 0.0)
            cqp[pl.ds(r, 8, stride=16), :] = dq[:, 0:128]
            cqp[pl.ds(r + 1, 8, stride=16), :] = dq[:, 128:256]
            pq = dens * q8
            dout = dens * c8
            dsum = dsum + dout
            ph, pw = high_low(pq)
            dh, dl = high_low(dout)
            left = jnp.concatenate([ph, pw, dh, dl], axis=0).astype(BF16)
            right = jnp.concatenate([thb, tlb, hhb, hlb], axis=0)
            acc = acc + lax.dot_general(left, right, (((1,), (1,)), ((), ())), preferred_element_type=F32)
        a = acc[0:8, 0:128]
        a = a + pltpu.roll(a, 64, 1) + acc[8:16, 0:128]
        b = acc[16:24, 128:256]
        b = b + pltpu.roll(b, 64, 1) + acc[24:32, 128:256]
        total = jnp.where(lane < 64, a, pltpu.roll(b, 64, 1))
        d = jnp.sum(dsum[:, 0:128] + dsum[:, 128:256], axis=1, keepdims=True)
        d = jnp.sum(jnp.where(lane == row, d, 0.0), axis=0, keepdims=True)
        return jnp.where(row == 6, d, total)

    def flux_back(qp, cp, xq, xc, yq, yc, speed, after):
        speed8 = jnp.broadcast_to(speed, (8, 128))
        speed16 = jnp.broadcast_to(speed, (16, 128))
        speed256 = jnp.concatenate([speed8, speed8], axis=1)
        hx = [x_halo(xq, f) for f in range(5)]
        cx = [x_halo(xc, f) for f in range(5)]
        pq, pc = y_packed(yq), y_packed(yc)
        for z in range(2):
            own = [tile(qp, f, z) for f in range(5)]
            q = [jnp.concatenate([own[f], hx[f][z]], axis=0) for f in range(5)]
            for f, part in enumerate(flux_parts(q, 0)):
                lead = speed16 * q[f]
                fxp[2 * f + z] = 0.5 * (part + lead)
                fxm[2 * f + z] = 0.5 * (part - lead)
            q = [jnp.concatenate([own[f], y_halo(pq, f, z)], axis=1) for f in range(5)]
            for f, part in enumerate(flux_parts(q, 1)):
                lead = speed256 * q[f]
                fyp[2 * f + z] = 0.5 * (part + lead)
                fym[2 * f + z] = 0.5 * (part - lead)
            for f in range(5):
                t = 2 * f + z
                v = tile(cp, f, z)
                vx[t, 0:8, :] = v
                vx[t, 8:16, :] = cx[f][z]
                vy[t, :, 0:128] = v
                vy[t, :, 128:256] = y_halo(pc, f, z)

        def body(t, _):
            total, apart, laplace = line_adjoint(fxp[t], fxm[t], vx[t], 0, lambda x: x[0:8, :])
            gx_s[t] = 0.5 * total
            total_y, apart_y, laplace_y = line_adjoint(fyp[t], fym[t], vy[t], 1, lambda x: x[:, 0:128])
            gy_s[t] = 0.5 * total_y
            viscous = jnp.where(t < 2, 0.0, VISCOSITY).astype(F32)
            gq_s[t] = 0.5 * speed8 * (apart + apart_y) + viscous * (laplace + laplace_y)
            return 0

        lax.fori_loop(0, 10, body, 0)

        for z in range(2):
            q = [tile(qp, f, z) for f in range(5)]
            inv = 1.0 / q[0]
            vel = [None] + [q[j] * inv for j in (1, 2, 3)]
            square = vel[1] * vel[1] + vel[2] * vel[2] + vel[3] * vel[3]
            pressure = (GAMMA - 1.0) * (q[4] - 0.5 * q[0] * square)
            out = [gq_s[2 * f + z] for f in range(5)]
            for k, store in ((0, gx_s), (1, gy_s)):
                g = [store[2 * f + z] for f in range(5)]
                u = vel[k + 1]
                dp = (GAMMA - 1.0) * (g[k + 1] + g[4] * u)
                du = (g[1] * q[1] + g[2] * q[2] + g[3] * q[3] + g[4] * (q[4] + pressure)) * inv
                out[0] = out[0] - du * u + 0.5 * dp * square
                for j in (1, 2, 3):
                    out[j] = out[j] + g[j] * u - dp * vel[j]
                out[k + 1] = out[k + 1] + g[0] + du
                out[4] = out[4] + g[4] * u + dp
            for f in range(5):
                after(f, z, out[f] + tile(cqp, f, z))

    grads_one = closure_back(q1p, ctp)

    for s in range(len(stages)):
        speeds = end_stage(spd, s, spd_copies, jnp.maximum)
        if s + 1 < len(stages):
            spd_copies = begin_stage(spd, gsend, grecv, s + 1, speeds)
    for c in a_copies:
        c.wait_recv()

    def keep_middle(f, z, value):
        base = f * 16 + z * 8
        gmp[base : base + 8, :] = 0.25 * tile(ctp, f, z) + 0.25 * TIME_STEP * value

    flux_back(q1p, ctp, 0, 5, 0, 1, speeds[:, 128:256], keep_middle)
    pack(gmp, 15, 3)
    start(c_copies)

    grads_zero = closure_back(q0p, gmp)
    cells = 2 * 8 * 128 * GX * GY * AF
    params = (0.25 * TIME_STEP * grads_one + TIME_STEP * grads_zero) * (1.0 / cells)
    prm_copies = begin_stage(prm, psend, precv, 0, params)

    for c in b_copies + c_copies:
        c.wait_recv()

    def keep_state(f, z, value):
        base = f * 16 + z * 8
        out_ref[base : base + 8, :] = (
            0.75 * tile(ctp, f, z) + tile(gmp, f, z) + TIME_STEP * value
        )

    flux_back(q0p, gmp, 10, 15, 2, 3, speeds[:, 0:128], keep_state)

    for s in range(len(stages)):
        params = end_stage(prm, s, prm_copies, jnp.add)
        if s + 1 < len(stages):
            prm_copies = begin_stage(prm, psend, precv, s + 1, params)
    turned = jnp.transpose(jnp.concatenate([params, jnp.zeros((120, 128), F32)], axis=0))
    gwin_ref[...] = turned[0:64, 0:5]
    gbin_ref[...] = params[5:6, 0:64]
    gbout_ref[...] = params[6:7, 0:5]
    gwout_ref[...] = pltpu.roll(params, 64, 1)[0:5, 0:64]

    for c in started:
        c.wait_send()


def solution(mesh):
    sizes = (mesh.shape["gx"], mesh.shape["gy"], mesh.shape["af"])
    group = sum(sizes) if sizes[0] * sizes[1] * sizes[2] > 16 else sizes[0] * sizes[1] * sizes[2]

    def shards(s0, s1, ct, win, b_in, wout, b_out):
        shape = s0.shape
        vmem = pl.BlockSpec(memory_space=pltpu.VMEM)
        big = pltpu.VMEM((128, 128), F32)
        dma = pltpu.SemaphoreType.DMA
        out, gwin, gbin, gwout, gbout = pl.pallas_call(
            functools.partial(kernel, sizes),
            out_shape=(
                jax.ShapeDtypeStruct((80, 128), F32),
                jax.ShapeDtypeStruct((64, 5), F32),
                jax.ShapeDtypeStruct((1, 64), F32),
                jax.ShapeDtypeStruct((5, 64), F32),
                jax.ShapeDtypeStruct((1, 5), F32),
            ),
            in_specs=[vmem] * 7,
            out_specs=(vmem,) * 5,
            scratch_shapes=[
                big, big, big, big, big, big,
                pltpu.VMEM((64, 32), BF16),
                pltpu.VMEM((64, 32), BF16),
                pltpu.VMEM((16, 256), BF16),
                pltpu.VMEM((8, 128), F32),
                pltpu.VMEM((10, 16, 128), F32),
                pltpu.VMEM((10, 16, 128), F32),
                pltpu.VMEM((10, 8, 256), F32),
                pltpu.VMEM((10, 8, 256), F32),
                pltpu.VMEM((10, 16, 128), F32),
                pltpu.VMEM((10, 8, 256), F32),
                pltpu.VMEM((10, 8, 128), F32),
                pltpu.VMEM((10, 8, 128), F32),
                pltpu.VMEM((10, 8, 128), F32),
                pltpu.VMEM((2, 20, 8, 128), F32),
                pltpu.VMEM((2, 20, 8, 128), F32),
                pltpu.VMEM((4, 8, 128), F32),
                pltpu.VMEM((2, 4, 8, 128), F32),
                pltpu.VMEM((group, 1, 256), F32),
                pltpu.VMEM((group, 8, 128), F32),
                dma((2, 3)), dma((2, 3)), dma((2, 3)), dma((2, 3)),
                dma((group,)), dma((group,)), dma((group,)), dma((group,)),
            ],
            compiler_params=pltpu.CompilerParams(
                collective_id=0, has_side_effects=True, vmem_limit_bytes=32 * 1024 * 1024
            ),
            name="adjoint",
        )(
            s0.reshape(80, 128), s1.reshape(80, 128), ct.reshape(80, 128),
            win, b_in.reshape(1, 64), wout, b_out.reshape(1, 5),
        )
        return out.reshape(shape), gwin, gbin.reshape(64), gwout, gbout.reshape(5)

    field = P(None, "af", ("cases", "gx"), "gy")
    return jax.shard_map(
        shards,
        mesh=mesh,
        in_specs=(field, field, field, P(), P(), P(), P()),
        out_specs=(field, P("cases", None), P("cases"), P("cases", None), P("cases")),
        check_vma=False,
    )
```

```python
import functools

import jax
import jax.numpy as jnp
from jax import lax
from jax.experimental import pallas as pl
from jax.experimental.pallas import tpu as pltpu
from jax.sharding import PartitionSpec as P

MESH = pl.DeviceIdType.MESH
GAMMA = 1.4
TIME_STEP = 0.1
VISCOSITY = 0.2
WENO_EPS = 1e-06
F32 = jnp.float32
BF16 = jnp.bfloat16


def shifted(x, by, axis):
    return pltpu.roll(x, (-by) % x.shape[axis], axis)


def high_low(x):
    high = x.astype(BF16).astype(F32)
    return high, x - high


def inverse(x):
    return pl.reciprocal(x, approx=True)


def weno_grads(d0, d1, d2, d3):
    a0 = 8.0 * d0 - 11.0 * d1
    a1 = 20.0 * d1 - 11.0 * d0
    b0 = 8.0 * d1 - 5.0 * d2
    b1 = 8.0 * d2 - 5.0 * d1
    c0 = 20.0 * d2 - 11.0 * d3
    c1 = 8.0 * d3 - 11.0 * d2
    eps = 6.0 * WENO_EPS
    ra = inverse(eps + (d0 * a0 + d1 * a1))
    rb = inverse(eps + (d1 * b0 + d2 * b1))
    rc = inverse(eps + (d2 * c0 + d3 * c1))
    wa = ra * ra
    wb = 6.0 * (rb * rb)
    wc = 3.0 * (rc * rc)
    ga = 5.0 * d1 - 2.0 * d0
    gb = d1 + 2.0 * d2
    gc = 4.0 * d2 - d3
    inv = inverse(wa + wb + wc)
    mean = (wa * ga + wb * gb + wc * gc) * inv
    ka = wa * inv
    kb = wb * inv
    kc = wc * inv
    ma = 4.0 * ka * ra * (mean - ga)
    mb = 4.0 * kb * rb * (mean - gb)
    mc = 4.0 * kc * rc * (mean - gc)
    return (
        ma * a0 - 2.0 * ka,
        ma * a1 + 5.0 * ka + mb * b0 + kb,
        mb * b1 + 2.0 * kb + mc * c0 + 4.0 * kc,
        mc * c1 - kc,
    )


def line_grads(up, down, axis):
    sh = functools.partial(shifted, axis=axis)
    d = sh(up, 1) - up
    e = down - sh(down, 1)
    return weno_grads(sh(d, -2), sh(d, -1), d, sh(d, 1)), weno_grads(sh(e, 2), sh(e, 1), e, sh(e, -1))


def line_adjoint(grads, v, axis, own):
    sh = functools.partial(shifted, axis=axis)
    ahead = sh(v, 1)
    w = ahead - v
    w6 = w * (1.0 / 6.0)
    wb = sh(w, -1)
    g = [w6 * x for x in grads[0]]
    gp = sh(sh(g[0], 1) + g[1], 1) + g[2] + sh(g[3], -1)
    g = [w6 * x for x in grads[1]]
    gm = sh(sh(g[0], -1) + g[1], -1) + g[2] + sh(g[3], 1)
    t = gp - gm
    s = gp + gm
    total = w + wb + sh(t, -1) - t
    apart = w - wb + sh(s, -1) - s
    return own(total), own(apart), own(w - wb)


def flux_parts(q, k):
    inv = inverse(q[0])
    pressure = (GAMMA - 1.0) * (
        q[4] - 0.5 * (q[1] * q[1] + q[2] * q[2] + q[3] * q[3]) * inv
    )
    u = q[k + 1] * inv
    f = [q[k + 1], q[1] * u, q[2] * u, q[3] * u, (q[4] + pressure) * u]
    f[k + 1] = f[k + 1] + pressure
    return f


def kernel(
    sizes,
    s0_ref, s1_ref, ct_ref, win_ref, bin_ref, wout_ref, bout_ref,
    out_ref, gwin_ref, gbin_ref, gwout_ref, gbout_ref,
    q0p, q1p, ctp, gmp, cqp, wtile, w1, w2, w3, bcol,
    fxp, fxm, fyp, fym, kx, ky, vx, vy, gx_s, gy_s, gq_s,
    xs, xr, ys, yr, spd, prm,
    xsend, xrecv, ysend, yrecv, gsend, grecv, psend, precv,
):
    GX, GY, AF = sizes
    ix, iy, ia = lax.axis_index("gx"), lax.axis_index("gy"), lax.axis_index("af")
    ic = lax.axis_index("cases")
    joint = GX * GY * AF <= 16
    if joint:
        stages = [[(a, b, c) for a in range(GX) for b in range(GY) for c in range(AF)]]
    else:
        stages = [
            [(a, 0, 0) for a in range(GX)],
            [(0, b, 0) for b in range(GY)],
            [(0, 0, c) for c in range(AF)],
        ]

    def place(off):
        return (
            ic,
            lax.rem(ix + off[0], GX) if off[0] else ix,
            lax.rem(iy + off[1], GY) if off[1] else iy,
            lax.rem(ia + off[2], AF) if off[2] else ia,
        )

    barrier = pltpu.get_barrier_semaphore()
    greeted = 0
    for stage in stages:
        for off in stage[1:]:
            pl.semaphore_signal(barrier, inc=1, device_id=place(off), device_id_type=MESH)
            greeted += 1

    row = lax.broadcasted_iota(jnp.int32, (8, 128), 0)
    lane = lax.broadcasted_iota(jnp.int32, (8, 128), 1)
    upper = row < 4

    ones = jnp.ones((16, 128), F32)
    for ref, src in ((q0p, s0_ref), (q1p, s1_ref), (ctp, ct_ref)):
        ref[0:80, :] = src[...]
    for ref in (q0p, q1p):
        ref[80:96, :] = ones
        ref[96:128, :] = jnp.zeros((32, 128), F32)
    for ref in (ctp, gmp):
        ref[80:128, :] = jnp.zeros((48, 128), F32)

    def tile(ref, f, z):
        return ref[f * 16 + z * 8 : f * 16 + z * 8 + 8, :]

    def pack(ref, base, yslot):
        packed = jnp.zeros((8, 128), F32)
        for f in range(5):
            one, two = tile(ref, f, 0), pltpu.roll(tile(ref, f, 1), 4, 0)
            xs[0, base + f] = jnp.where(upper, one, two)
            xs[1, base + f] = jnp.where(upper, two, one)
            for z in range(2):
                t = f * 2 + z
                moved = pltpu.roll(tile(ref, f, z), (4 + 8 * t) % 128, 1)
                packed = jnp.where((lane >= 8 * t) & (lane < 8 * t + 8), moved, packed)
        ys[yslot] = packed

    def x_copies(base, count, sem):
        made = []
        for way in range(2):
            off = (GX - 1, 0, 0) if way == 0 else (1, 0, 0)
            made.append(
                pltpu.make_async_remote_copy(
                    src_ref=xs.at[way, pl.ds(base, count)],
                    dst_ref=xr.at[way, pl.ds(base, count)],
                    send_sem=xsend.at[way, sem],
                    recv_sem=xrecv.at[way, sem],
                    device_id=place(off),
                    device_id_type=MESH,
                )
            )
        return made

    def y_copies(base, count, sem):
        made = []
        for way in range(1 if GY == 2 else 2):
            off = (0, 1, 0) if way == 0 else (0, GY - 1, 0)
            made.append(
                pltpu.make_async_remote_copy(
                    src_ref=ys.at[pl.ds(base, count)],
                    dst_ref=yr.at[way, pl.ds(base, count)],
                    send_sem=ysend.at[way, sem],
                    recv_sem=yrecv.at[way, sem],
                    device_id=place(off),
                    device_id_type=MESH,
                )
            )
        return made

    def x_halo(base, f):
        ahead, behind = xr[0, base + f], xr[1, base + f]
        return (
            jnp.where(upper, ahead, behind),
            pltpu.roll(jnp.where(upper, behind, ahead), 4, 0),
        )

    def y_packed(slot):
        if GY == 2:
            return yr[0, slot]
        return jnp.where(lax.rem(lane, 8) < 4, yr[0, slot], yr[1, slot])

    def y_halo(packed, f, z):
        return pltpu.roll(packed, (-(4 + 8 * (f * 2 + z))) % 128, 1)

    pack(q1p, 0, 0)
    pack(ctp, 5, 1)
    pack(q0p, 10, 2)

    def top_speed(ref):
        best = None
        for z in range(2):
            q = [tile(ref, f, z) for f in range(5)]
            inv = inverse(q[0])
            pressure = (GAMMA - 1.0) * (
                q[4] - 0.5 * (q[1] * q[1] + q[2] * q[2] + q[3] * q[3]) * inv
            )
            sound = jnp.sqrt(GAMMA * pressure * inv)
            value = jnp.maximum(jnp.abs(q[1] * inv), jnp.abs(q[2] * inv)) + sound
            best = value if best is None else jnp.maximum(best, value)
        best = jnp.max(best, axis=0, keepdims=True)
        return jnp.broadcast_to(jnp.max(best, axis=1, keepdims=True), (1, 128))

    fastest = jnp.concatenate([top_speed(q0p), top_speed(q1p)], axis=1)

    wtile[...] = jnp.zeros_like(wtile)
    wtile[0:64, 0:5] = win_ref[...]
    wint = jnp.transpose(wtile[...])[0:8, :]
    wtile[0:8, :] = jnp.zeros((8, 128), F32)
    wtile[0:5, 0:64] = wout_ref[...]
    wout8 = wtile[0:8, :]
    wtile[0:8, :] = jnp.zeros((8, 128), F32)
    wtile[0:1, 0:64] = bin_ref[...]
    wtile[1:2, 0:5] = bout_ref[...]
    bin_row = wtile[0:1, :]
    bout_row = wtile[1:2, :]
    aug = jnp.where(row == 5, bin_row, wint)
    zero8 = jnp.zeros((8, 128), F32)
    ah, al = high_low(aug)
    oh, ol = high_low(wout8)
    fill = jnp.zeros((96, 128), F32)
    w1[...] = jnp.transpose(jnp.concatenate([ah, ah, al, zero8, fill], axis=0))[0:64, 0:32].astype(BF16)
    w2[...] = jnp.transpose(jnp.concatenate([oh, oh, ol, zero8, fill], axis=0))[0:64, 0:32].astype(BF16)
    ih, il = high_low(wint)
    lo_lane = lane < 64
    first = jnp.where(lo_lane, ih, pltpu.roll(ih, 64, 1))
    w3[:, 0:128] = jnp.concatenate([first, zero8], axis=0).astype(BF16)
    w3[:, 128:256] = jnp.concatenate([jnp.where(lo_lane, il, 0.0), zero8], axis=0).astype(BF16)
    bcol[...] = jnp.broadcast_to(
        jnp.sum(jnp.where(lane == row, jnp.broadcast_to(bout_row, (8, 128)), 0.0), axis=1, keepdims=True),
        (8, 128),
    )

    pl.semaphore_wait(barrier, greeted)

    a_copies = x_copies(0, 10, 0) + y_copies(0, 2, 0)
    b_copies = x_copies(10, 5, 1) + y_copies(2, 1, 1)
    c_copies = x_copies(15, 5, 2) + y_copies(3, 1, 2)

    def numbers(stage_index):
        base = sum(len(stages[s]) for s in range(stage_index))
        return [base + k for k in range(len(stages[stage_index]))]

    def my_rank(stage_index):
        if joint:
            return (ix * GY + iy) * AF + ia
        return (ix, iy, ia)[stage_index]

    def group_copies(buf, send, recv, stage_index):
        base = numbers(stage_index)[0]
        rank = base + my_rank(stage_index)
        made = []
        for k, off in enumerate(stages[stage_index]):
            if k == 0:
                continue
            made.append(
                pltpu.make_async_remote_copy(
                    src_ref=buf.at[rank],
                    dst_ref=buf.at[rank],
                    send_sem=send.at[base + k],
                    recv_sem=recv.at[base + k],
                    device_id=place(off),
                    device_id_type=MESH,
                )
            )
        return made

    started = []

    def start(copies):
        for c in copies:
            c.start()
            started.append(c)

    def begin_stage(buf, send, recv, s, value):
        buf[numbers(s)[0] + my_rank(s)] = value
        copies = group_copies(buf, send, recv, s)
        start(copies)
        return copies

    def end_stage(buf, s, copies, op):
        for c in copies:
            c.wait_recv()
        total = None
        for n in numbers(s):
            total = buf[n] if total is None else op(total, buf[n])
        return total

    spd_copies = begin_stage(spd, gsend, grecv, 0, fastest)
    start(a_copies)
    start(b_copies)

    def closure_back(qp, cp):
        acc = jnp.zeros((32, 256), F32)
        dsum = jnp.zeros((8, 256), F32)
        bb = jnp.concatenate([bcol[...], bcol[...]], axis=1)
        for chunk in range(8):
            r = 2 * chunk
            q8 = jnp.concatenate([qp[pl.ds(r, 8, stride=16), :], qp[pl.ds(r + 1, 8, stride=16), :]], axis=1)
            c8 = jnp.concatenate([cp[pl.ds(r, 8, stride=16), :], cp[pl.ds(r + 1, 8, stride=16), :]], axis=1)
            zero = jnp.zeros((8, 256), F32)
            qh, ql = high_low(q8)
            ch, cl = high_low(c8)
            pre = jnp.dot(w1[...], jnp.concatenate([qh, ql, qh, zero], axis=0).astype(BF16), preferred_element_type=F32)
            g = jnp.dot(w2[...], jnp.concatenate([ch, cl, ch, zero], axis=0).astype(BF16), preferred_element_type=F32)
            h = jnp.tanh(pre)
            t = g * (1.0 - h * h)
            hg = bb * c8
            prod = h * g
            for k in range(8):
                hg = hg + prod[8 * k : 8 * k + 8, :]
            hg = jnp.sum(hg, axis=0, keepdims=True)
            th, tl = high_low(t)
            hh, hl = high_low(h)
            thb, tlb = th.astype(BF16), tl.astype(BF16)
            hhb, hlb = hh.astype(BF16), hl.astype(BF16)
            stack = jnp.concatenate([thb, tlb, thb, jnp.zeros((64, 256), BF16)], axis=0)
            dq = jnp.dot(w3[...], stack, preferred_element_type=F32)[0:8, :]
            dens = q8[0:1, :]
            row2 = lax.broadcasted_iota(jnp.int32, (8, 256), 0)
            dq = dens * dq + jnp.where(row2 == 0, hg, 0.0)
            cqp[pl.ds(r, 8, stride=16), :] = dq[:, 0:128]
            cqp[pl.ds(r + 1, 8, stride=16), :] = dq[:, 128:256]
            pq = dens * q8
            dout = dens * c8
            dsum = dsum + dout
            ph, pw = high_low(pq)
            dh, dl = high_low(dout)
            left = jnp.concatenate([ph, pw, dh, dl], axis=0).astype(BF16)
            right = jnp.concatenate([thb, tlb, hhb, hlb], axis=0)
            acc = acc + lax.dot_general(left, right, (((1,), (1,)), ((), ())), preferred_element_type=F32)
        a = acc[0:8, 0:128]
        a = a + pltpu.roll(a, 64, 1) + acc[8:16, 0:128]
        b = acc[16:24, 128:256]
        b = b + pltpu.roll(b, 64, 1) + acc[24:32, 128:256]
        total = jnp.where(lane < 64, a, pltpu.roll(b, 64, 1))
        d = jnp.sum(dsum[:, 0:128] + dsum[:, 128:256], axis=1, keepdims=True)
        d = jnp.sum(jnp.where(lane == row, d, 0.0), axis=0, keepdims=True)
        return jnp.where(row == 6, d, total)

    def flux_parts_of(qp, xq, yq, speed):
        speed8 = jnp.broadcast_to(speed, (8, 128))
        speed16 = jnp.broadcast_to(speed, (16, 128))
        speed256 = jnp.concatenate([speed8, speed8], axis=1)
        hx = [x_halo(xq, f) for f in range(5)]
        pq = y_packed(yq)
        for z in range(2):
            own = [tile(qp, f, z) for f in range(5)]
            q = [jnp.concatenate([own[f], hx[f][z]], axis=0) for f in range(5)]
            for f, part in enumerate(flux_parts(q, 0)):
                lead = speed16 * q[f]
                fxp[2 * f + z] = 0.5 * (part + lead)
                fxm[2 * f + z] = 0.5 * (part - lead)
            q = [jnp.concatenate([own[f], y_halo(pq, f, z)], axis=1) for f in range(5)]
            for f, part in enumerate(flux_parts(q, 1)):
                lead = speed256 * q[f]
                fyp[2 * f + z] = 0.5 * (part + lead)
                fym[2 * f + z] = 0.5 * (part - lead)

    def fill_v(cp, xc, yc):
        pc = y_packed(yc)
        for f in range(5):
            hx = x_halo(xc, f)
            for z in range(2):
                t = 2 * f + z
                v = tile(cp, f, z)
                vx[t, 0:8, :] = v
                vx[t, 8:16, :] = hx[z]
                vy[t, :, 0:128] = v
                vy[t, :, 128:256] = y_halo(pc, f, z)

    def grads_of(t):
        return line_grads(fxp[t], fxm[t], 0), line_grads(fyp[t], fym[t], 1)

    def keep_grads(t, _):
        along_x, along_y = grads_of(t)
        for side in range(2):
            for k in range(4):
                kx[t, side, k] = along_x[side][k]
                ky[t, side, k] = along_y[side][k]
        return 0

    def kept_grads(t):
        return (
            [[kx[t, side, k] for k in range(4)] for side in range(2)],
            [[ky[t, side, k] for k in range(4)] for side in range(2)],
        )

    def flux_back(qp, grads_at, speed, after):
        speed8 = jnp.broadcast_to(speed, (8, 128))

        def body(t, _):
            along_x, along_y = grads_at(t)
            total, apart, laplace = line_adjoint(along_x, vx[t], 0, lambda x: x[0:8, :])
            gx_s[t] = 0.5 * total
            total_y, apart_y, laplace_y = line_adjoint(along_y, vy[t], 1, lambda x: x[:, 0:128])
            gy_s[t] = 0.5 * total_y
            viscous = jnp.where(t < 2, 0.0, VISCOSITY).astype(F32)
            gq_s[t] = 0.5 * speed8 * (apart + apart_y) + viscous * (laplace + laplace_y)
            return 0

        lax.fori_loop(0, 10, body, 0)

        for z in range(2):
            q = [tile(qp, f, z) for f in range(5)]
            inv = inverse(q[0])
            vel = [None] + [q[j] * inv for j in (1, 2, 3)]
            square = vel[1] * vel[1] + vel[2] * vel[2] + vel[3] * vel[3]
            pressure = (GAMMA - 1.0) * (q[4] - 0.5 * q[0] * square)
            out = [gq_s[2 * f + z] for f in range(5)]
            for k, store in ((0, gx_s), (1, gy_s)):
                g = [store[2 * f + z] for f in range(5)]
                u = vel[k + 1]
                dp = (GAMMA - 1.0) * (g[k + 1] + g[4] * u)
                du = (g[1] * q[1] + g[2] * q[2] + g[3] * q[3] + g[4] * (q[4] + pressure)) * inv
                out[0] = out[0] - du * u + 0.5 * dp * square
                for j in (1, 2, 3):
                    out[j] = out[j] + g[j] * u - dp * vel[j]
                out[k + 1] = out[k + 1] + g[0] + du
                out[4] = out[4] + g[4] * u + dp
            for f in range(5):
                after(f, z, out[f] + tile(cqp, f, z))

    grads_one = closure_back(q1p, ctp)

    for s in range(len(stages)):
        speeds = end_stage(spd, s, spd_copies, jnp.maximum)
        if s + 1 < len(stages):
            spd_copies = begin_stage(spd, gsend, grecv, s + 1, speeds)
    for c in a_copies:
        c.wait_recv()

    def keep_middle(f, z, value):
        base = f * 16 + z * 8
        gmp[base : base + 8, :] = 0.25 * tile(ctp, f, z) + 0.25 * TIME_STEP * value

    flux_parts_of(q1p, 0, 0, speeds[:, 128:256])
    fill_v(ctp, 5, 1)
    flux_back(q1p, grads_of, speeds[:, 128:256], keep_middle)
    pack(gmp, 15, 3)
    start(c_copies)

    grads_zero = closure_back(q0p, gmp)
    cells = 2 * 8 * 128 * GX * GY * AF
    params = (0.25 * TIME_STEP * grads_one + TIME_STEP * grads_zero) * (1.0 / cells)
    prm_copies = begin_stage(prm, psend, precv, 0, params)

    for c in b_copies:
        c.wait_recv()
    flux_parts_of(q0p, 10, 2, speeds[:, 0:128])
    lax.fori_loop(0, 10, keep_grads, 0)
    for c in c_copies:
        c.wait_recv()
    fill_v(gmp, 15, 3)

    def keep_state(f, z, value):
        base = f * 16 + z * 8
        out_ref[base : base + 8, :] = (
            0.75 * tile(ctp, f, z) + tile(gmp, f, z) + TIME_STEP * value
        )

    flux_back(q0p, kept_grads, speeds[:, 0:128], keep_state)

    for s in range(len(stages)):
        params = end_stage(prm, s, prm_copies, jnp.add)
        if s + 1 < len(stages):
            prm_copies = begin_stage(prm, psend, precv, s + 1, params)
    turned = jnp.transpose(jnp.concatenate([params, jnp.zeros((120, 128), F32)], axis=0))
    gwin_ref[...] = turned[0:64, 0:5]
    gbin_ref[...] = params[5:6, 0:64]
    gbout_ref[...] = params[6:7, 0:5]
    gwout_ref[...] = pltpu.roll(params, 64, 1)[0:5, 0:64]

    for c in started:
        c.wait_send()


def solution(mesh):
    sizes = (mesh.shape["gx"], mesh.shape["gy"], mesh.shape["af"])
    group = sum(sizes) if sizes[0] * sizes[1] * sizes[2] > 16 else sizes[0] * sizes[1] * sizes[2]

    def shards(s0, s1, ct, win, b_in, wout, b_out):
        shape = s0.shape
        vmem = pl.BlockSpec(memory_space=pltpu.VMEM)
        big = pltpu.VMEM((128, 128), F32)
        dma = pltpu.SemaphoreType.DMA
        out, gwin, gbin, gwout, gbout = pl.pallas_call(
            functools.partial(kernel, sizes),
            out_shape=(
                jax.ShapeDtypeStruct((80, 128), F32),
                jax.ShapeDtypeStruct((64, 5), F32),
                jax.ShapeDtypeStruct((1, 64), F32),
                jax.ShapeDtypeStruct((5, 64), F32),
                jax.ShapeDtypeStruct((1, 5), F32),
            ),
            in_specs=[vmem] * 7,
            out_specs=(vmem,) * 5,
            scratch_shapes=[
                big, big, big, big, big, big,
                pltpu.VMEM((64, 32), BF16),
                pltpu.VMEM((64, 32), BF16),
                pltpu.VMEM((16, 256), BF16),
                pltpu.VMEM((8, 128), F32),
                pltpu.VMEM((10, 16, 128), F32),
                pltpu.VMEM((10, 16, 128), F32),
                pltpu.VMEM((10, 8, 256), F32),
                pltpu.VMEM((10, 8, 256), F32),
                pltpu.VMEM((10, 2, 4, 16, 128), F32),
                pltpu.VMEM((10, 2, 4, 8, 256), F32),
                pltpu.VMEM((10, 16, 128), F32),
                pltpu.VMEM((10, 8, 256), F32),
                pltpu.VMEM((10, 8, 128), F32),
                pltpu.VMEM((10, 8, 128), F32),
                pltpu.VMEM((10, 8, 128), F32),
                pltpu.VMEM((2, 20, 8, 128), F32),
                pltpu.VMEM((2, 20, 8, 128), F32),
                pltpu.VMEM((4, 8, 128), F32),
                pltpu.VMEM((2, 4, 8, 128), F32),
                pltpu.VMEM((group, 1, 256), F32),
                pltpu.VMEM((group, 8, 128), F32),
                dma((2, 3)), dma((2, 3)), dma((2, 3)), dma((2, 3)),
                dma((group,)), dma((group,)), dma((group,)), dma((group,)),
            ],
            compiler_params=pltpu.CompilerParams(
                collective_id=0, has_side_effects=True, vmem_limit_bytes=32 * 1024 * 1024
            ),
            name="adjoint",
        )(
            s0.reshape(80, 128), s1.reshape(80, 128), ct.reshape(80, 128),
            win, b_in.reshape(1, 64), wout, b_out.reshape(1, 5),
        )
        return out.reshape(shape), gwin, gbin.reshape(64), gwout, gbout.reshape(5)

    field = P(None, "af", ("cases", "gx"), "gy")
    return jax.shard_map(
        shards,
        mesh=mesh,
        in_specs=(field, field, field, P(), P(), P(), P()),
        out_specs=(field, P("cases", None), P("cases"), P("cases", None), P("cases")),
        check_vma=False,
    )
```

```python
import functools

import jax
import jax.numpy as jnp
from jax import lax
from jax.experimental import pallas as pl
from jax.experimental.pallas import tpu as pltpu
from jax.sharding import PartitionSpec as P

MESH = pl.DeviceIdType.MESH
GAMMA = 1.4
TIME_STEP = 0.1
VISCOSITY = 0.2
WENO_EPS = 1e-06
F32 = jnp.float32
BF16 = jnp.bfloat16


def shifted(x, by, axis):
    return pltpu.roll(x, (-by) % x.shape[axis], axis)


def high_low(x):
    high = x.astype(BF16).astype(F32)
    return high, x - high


def inverse(x):
    return pl.reciprocal(x, approx=True)


def weno_grads(d0, d1, d2, d3):
    a0 = 8.0 * d0 - 11.0 * d1
    a1 = 20.0 * d1 - 11.0 * d0
    b0 = 8.0 * d1 - 5.0 * d2
    b1 = 8.0 * d2 - 5.0 * d1
    c0 = 20.0 * d2 - 11.0 * d3
    c1 = 8.0 * d3 - 11.0 * d2
    eps = 6.0 * WENO_EPS
    ra = inverse(eps + (d0 * a0 + d1 * a1))
    rb = inverse(eps + (d1 * b0 + d2 * b1))
    rc = inverse(eps + (d2 * c0 + d3 * c1))
    wa = ra * ra
    wb = 6.0 * (rb * rb)
    wc = 3.0 * (rc * rc)
    ga = 5.0 * d1 - 2.0 * d0
    gb = d1 + 2.0 * d2
    gc = 4.0 * d2 - d3
    inv = inverse(wa + wb + wc)
    mean = (wa * ga + wb * gb + wc * gc) * inv
    ka = wa * inv
    kb = wb * inv
    kc = wc * inv
    ma = 4.0 * ka * ra * (mean - ga)
    mb = 4.0 * kb * rb * (mean - gb)
    mc = 4.0 * kc * rc * (mean - gc)
    return (
        ma * a0 - 2.0 * ka,
        ma * a1 + 5.0 * ka + mb * b0 + kb,
        mb * b1 + 2.0 * kb + mc * c0 + 4.0 * kc,
        mc * c1 - kc,
    )


def line_grads(up, down, axis):
    sh = functools.partial(shifted, axis=axis)
    d = sh(up, 1) - up
    e = down - sh(down, 1)
    return weno_grads(sh(d, -2), sh(d, -1), d, sh(d, 1)), weno_grads(sh(e, 2), sh(e, 1), e, sh(e, -1))


def line_adjoint(grads, v, axis, own):
    sh = functools.partial(shifted, axis=axis)
    ahead = sh(v, 1)
    w = ahead - v
    w6 = w * (1.0 / 6.0)
    wb = sh(w, -1)
    g = [w6 * x for x in grads[0]]
    gp = sh(sh(g[0], 1) + g[1], 1) + g[2] + sh(g[3], -1)
    g = [w6 * x for x in grads[1]]
    gm = sh(sh(g[0], -1) + g[1], -1) + g[2] + sh(g[3], 1)
    t = gp - gm
    s = gp + gm
    total = w + wb + sh(t, -1) - t
    apart = w - wb + sh(s, -1) - s
    return own(total), own(apart), own(w - wb)


def flux_parts(q, k):
    inv = inverse(q[0])
    pressure = (GAMMA - 1.0) * (
        q[4] - 0.5 * (q[1] * q[1] + q[2] * q[2] + q[3] * q[3]) * inv
    )
    u = q[k + 1] * inv
    f = [q[k + 1], q[1] * u, q[2] * u, q[3] * u, (q[4] + pressure) * u]
    f[k + 1] = f[k + 1] + pressure
    return f


def kernel(
    sizes,
    s0_hbm, s1_hbm, ct_hbm, win_hbm, bin_hbm, wout_hbm, bout_hbm,
    out_ref,
    win_ref, bin_ref, wout_ref, bout_ref, in_sem,
    q0p, q1p, ctp, gmp, cqp, wtile, w1, w2, w3, bcol,
    fxp, fxm, fyp, fym, kx, ky, vx, vy, gx_s, gy_s, gq_s,
    xs, xr, ys, yr, spd, prm,
    xsend, xrecv, ysend, yrecv, gsend, grecv, psend, precv,
):
    GX, GY, AF = sizes
    ix, iy, ia = lax.axis_index("gx"), lax.axis_index("gy"), lax.axis_index("af")
    ic = lax.axis_index("cases")
    joint = GX * GY * AF <= 16
    if joint:
        stages = [[(a, b, c) for a in range(GX) for b in range(GY) for c in range(AF)]]
    else:
        stages = [
            [(a, 0, 0) for a in range(GX)],
            [(0, b, 0) for b in range(GY)],
            [(0, 0, c) for c in range(AF)],
        ]

    def place(off):
        return (
            ic,
            lax.rem(ix + off[0], GX) if off[0] else ix,
            lax.rem(iy + off[1], GY) if off[1] else iy,
            lax.rem(ia + off[2], AF) if off[2] else ia,
        )

    loads = []
    for n, (src, dst) in enumerate((
        (s1_hbm, q1p.at[0:80]), (ct_hbm, ctp.at[0:80]), (s0_hbm, q0p.at[0:80]),
        (win_hbm, win_ref), (bin_hbm, bin_ref), (wout_hbm, wout_ref), (bout_hbm, bout_ref),
    )):
        loads.append(pltpu.make_async_copy(src, dst, in_sem.at[n]))
        loads[-1].start()

    barrier = pltpu.get_barrier_semaphore()
    greeted = 0
    for stage in stages:
        for off in stage[1:]:
            pl.semaphore_signal(barrier, inc=1, device_id=place(off), device_id_type=MESH)
            greeted += 1

    row = lax.broadcasted_iota(jnp.int32, (8, 128), 0)
    lane = lax.broadcasted_iota(jnp.int32, (8, 128), 1)
    upper = row < 4

    ones = jnp.ones((16, 128), F32)
    for ref in (q0p, q1p):
        ref[80:96, :] = ones
        ref[96:128, :] = jnp.zeros((32, 128), F32)
    for ref in (ctp, gmp):
        ref[80:128, :] = jnp.zeros((48, 128), F32)

    def tile(ref, f, z):
        return ref[f * 16 + z * 8 : f * 16 + z * 8 + 8, :]

    def pack(ref, base, yslot):
        packed = jnp.zeros((8, 128), F32)
        for f in range(5):
            one, two = tile(ref, f, 0), pltpu.roll(tile(ref, f, 1), 4, 0)
            xs[0, base + f] = jnp.where(upper, one, two)
            xs[1, base + f] = jnp.where(upper, two, one)
            for z in range(2):
                t = f * 2 + z
                moved = pltpu.roll(tile(ref, f, z), (4 + 8 * t) % 128, 1)
                packed = jnp.where((lane >= 8 * t) & (lane < 8 * t + 8), moved, packed)
        ys[yslot] = packed

    def x_copies(base, count, sem):
        made = []
        for way in range(2):
            off = (GX - 1, 0, 0) if way == 0 else (1, 0, 0)
            made.append(
                pltpu.make_async_remote_copy(
                    src_ref=xs.at[way, pl.ds(base, count)],
                    dst_ref=xr.at[way, pl.ds(base, count)],
                    send_sem=xsend.at[way, sem],
                    recv_sem=xrecv.at[way, sem],
                    device_id=place(off),
                    device_id_type=MESH,
                )
            )
        return made

    def y_copies(base, count, sem):
        made = []
        for way in range(1 if GY == 2 else 2):
            off = (0, 1, 0) if way == 0 else (0, GY - 1, 0)
            made.append(
                pltpu.make_async_remote_copy(
                    src_ref=ys.at[pl.ds(base, count)],
                    dst_ref=yr.at[way, pl.ds(base, count)],
                    send_sem=ysend.at[way, sem],
                    recv_sem=yrecv.at[way, sem],
                    device_id=place(off),
                    device_id_type=MESH,
                )
            )
        return made

    def x_halo(base, f):
        ahead, behind = xr[0, base + f], xr[1, base + f]
        return (
            jnp.where(upper, ahead, behind),
            pltpu.roll(jnp.where(upper, behind, ahead), 4, 0),
        )

    def y_packed(slot):
        if GY == 2:
            return yr[0, slot]
        return jnp.where(lax.rem(lane, 8) < 4, yr[0, slot], yr[1, slot])

    def y_halo(packed, f, z):
        return pltpu.roll(packed, (-(4 + 8 * (f * 2 + z))) % 128, 1)

    loads[0].wait()
    pack(q1p, 0, 0)
    loads[1].wait()
    pack(ctp, 5, 1)
    loads[2].wait()
    pack(q0p, 10, 2)

    def top_speed(ref):
        best = None
        for z in range(2):
            q = [tile(ref, f, z) for f in range(5)]
            inv = inverse(q[0])
            pressure = (GAMMA - 1.0) * (
                q[4] - 0.5 * (q[1] * q[1] + q[2] * q[2] + q[3] * q[3]) * inv
            )
            sound = jnp.sqrt(GAMMA * pressure * inv)
            value = jnp.maximum(jnp.abs(q[1] * inv), jnp.abs(q[2] * inv)) + sound
            best = value if best is None else jnp.maximum(best, value)
        best = jnp.max(best, axis=0, keepdims=True)
        return jnp.broadcast_to(jnp.max(best, axis=1, keepdims=True), (1, 128))

    fastest = jnp.concatenate([top_speed(q0p), top_speed(q1p)], axis=1)

    wtile[0:8, :] = jnp.zeros((8, 128), F32)
    for c in loads[3:]:
        c.wait()
    wtile[0:5, 0:64] = win_ref[...]
    wint = wtile[0:8, :]
    wtile[0:5, 0:64] = wout_ref[...]
    wout8 = wtile[0:8, :]
    wtile[0:8, :] = jnp.zeros((8, 128), F32)
    wtile[0:1, 0:64] = bin_ref[...]
    wtile[1:2, 0:5] = bout_ref[...]
    bin_row = wtile[0:1, :]
    bout_row = wtile[1:2, :]
    aug = jnp.where(row == 5, bin_row, wint)
    zero8 = jnp.zeros((8, 128), F32)
    ah, al = high_low(aug)
    oh, ol = high_low(wout8)
    fill = jnp.zeros((96, 128), F32)
    w1[...] = jnp.transpose(jnp.concatenate([ah, ah, al, zero8, fill], axis=0))[0:64, 0:32].astype(BF16)
    w2[...] = jnp.transpose(jnp.concatenate([oh, oh, ol, zero8, fill], axis=0))[0:64, 0:32].astype(BF16)
    ih, il = high_low(wint)
    lo_lane = lane < 64
    first = jnp.where(lo_lane, ih, pltpu.roll(ih, 64, 1))
    w3[:, 0:128] = jnp.concatenate([first, zero8], axis=0).astype(BF16)
    w3[:, 128:256] = jnp.concatenate([jnp.where(lo_lane, il, 0.0), zero8], axis=0).astype(BF16)
    bcol[...] = jnp.broadcast_to(
        jnp.sum(jnp.where(lane == row, jnp.broadcast_to(bout_row, (8, 128)), 0.0), axis=1, keepdims=True),
        (8, 128),
    )

    pl.semaphore_wait(barrier, greeted)

    a_copies = x_copies(0, 10, 0) + y_copies(0, 2, 0)
    b_copies = x_copies(10, 5, 1) + y_copies(2, 1, 1)
    c_copies = x_copies(15, 5, 2) + y_copies(3, 1, 2)

    def numbers(stage_index):
        base = sum(len(stages[s]) for s in range(stage_index))
        return [base + k for k in range(len(stages[stage_index]))]

    def my_rank(stage_index):
        if joint:
            return (ix * GY + iy) * AF + ia
        return (ix, iy, ia)[stage_index]

    def group_copies(buf, send, recv, stage_index):
        base = numbers(stage_index)[0]
        rank = base + my_rank(stage_index)
        made = []
        for k, off in enumerate(stages[stage_index]):
            if k == 0:
                continue
            made.append(
                pltpu.make_async_remote_copy(
                    src_ref=buf.at[rank],
                    dst_ref=buf.at[rank],
                    send_sem=send.at[base + k],
                    recv_sem=recv.at[base + k],
                    device_id=place(off),
                    device_id_type=MESH,
                )
            )
        return made

    started = []

    def start(copies):
        for c in copies:
            c.start()
            started.append(c)

    def begin_stage(buf, send, recv, s, value):
        buf[numbers(s)[0] + my_rank(s)] = value
        copies = group_copies(buf, send, recv, s)
        start(copies)
        return copies

    def end_stage(buf, s, copies, op):
        for c in copies:
            c.wait_recv()
        total = None
        for n in numbers(s):
            total = buf[n] if total is None else op(total, buf[n])
        return total

    spd_copies = begin_stage(spd, gsend, grecv, 0, fastest)
    start(a_copies)
    start(b_copies)

    def closure_back(qp, cp):
        acc = jnp.zeros((32, 256), F32)
        dsum = jnp.zeros((8, 256), F32)
        bb = jnp.concatenate([bcol[...], bcol[...]], axis=1)
        for chunk in range(8):
            r = 2 * chunk
            q8 = jnp.concatenate([qp[pl.ds(r, 8, stride=16), :], qp[pl.ds(r + 1, 8, stride=16), :]], axis=1)
            c8 = jnp.concatenate([cp[pl.ds(r, 8, stride=16), :], cp[pl.ds(r + 1, 8, stride=16), :]], axis=1)
            zero = jnp.zeros((8, 256), F32)
            qh, ql = high_low(q8)
            ch, cl = high_low(c8)
            pre = jnp.dot(w1[...], jnp.concatenate([qh, ql, qh, zero], axis=0).astype(BF16), preferred_element_type=F32)
            g = jnp.dot(w2[...], jnp.concatenate([ch, cl, ch, zero], axis=0).astype(BF16), preferred_element_type=F32)
            h = jnp.tanh(pre)
            t = g * (1.0 - h * h)
            hg = bb * c8
            prod = h * g
            for k in range(8):
                hg = hg + prod[8 * k : 8 * k + 8, :]
            hg = jnp.sum(hg, axis=0, keepdims=True)
            th, tl = high_low(t)
            hh, hl = high_low(h)
            thb, tlb = th.astype(BF16), tl.astype(BF16)
            hhb, hlb = hh.astype(BF16), hl.astype(BF16)
            stack = jnp.concatenate([thb, tlb, thb, jnp.zeros((64, 256), BF16)], axis=0)
            dq = jnp.dot(w3[...], stack, preferred_element_type=F32)[0:8, :]
            dens = q8[0:1, :]
            row2 = lax.broadcasted_iota(jnp.int32, (8, 256), 0)
            dq = dens * dq + jnp.where(row2 == 0, hg, 0.0)
            cqp[pl.ds(r, 8, stride=16), :] = dq[:, 0:128]
            cqp[pl.ds(r + 1, 8, stride=16), :] = dq[:, 128:256]
            pq = dens * q8
            dout = dens * c8
            dsum = dsum + dout
            ph, pw = high_low(pq)
            dh, dl = high_low(dout)
            left = jnp.concatenate([ph, pw, dh, dl], axis=0).astype(BF16)
            right = jnp.concatenate([thb, tlb, hhb, hlb], axis=0)
            acc = acc + lax.dot_general(left, right, (((1,), (1,)), ((), ())), preferred_element_type=F32)
        a = acc[0:8, 0:128]
        a = a + pltpu.roll(a, 64, 1) + acc[8:16, 0:128]
        b = acc[16:24, 128:256]
        b = b + pltpu.roll(b, 64, 1) + acc[24:32, 128:256]
        total = jnp.where(lane < 64, a, pltpu.roll(b, 64, 1))
        d = jnp.sum(dsum[:, 0:128] + dsum[:, 128:256], axis=1, keepdims=True)
        d = jnp.sum(jnp.where(lane == row, d, 0.0), axis=0, keepdims=True)
        return jnp.where(row == 6, d, total)

    def flux_parts_of(qp, xq, yq, speed):
        speed8 = jnp.broadcast_to(speed, (8, 128))
        speed16 = jnp.broadcast_to(speed, (16, 128))
        speed256 = jnp.concatenate([speed8, speed8], axis=1)
        hx = [x_halo(xq, f) for f in range(5)]
        pq = y_packed(yq)
        for z in range(2):
            own = [tile(qp, f, z) for f in range(5)]
            q = [jnp.concatenate([own[f], hx[f][z]], axis=0) for f in range(5)]
            for f, part in enumerate(flux_parts(q, 0)):
                lead = speed16 * q[f]
                fxp[2 * f + z] = 0.5 * (part + lead)
                fxm[2 * f + z] = 0.5 * (part - lead)
            q = [jnp.concatenate([own[f], y_halo(pq, f, z)], axis=1) for f in range(5)]
            for f, part in enumerate(flux_parts(q, 1)):
                lead = speed256 * q[f]
                fyp[2 * f + z] = 0.5 * (part + lead)
                fym[2 * f + z] = 0.5 * (part - lead)

    def fill_v(cp, xc, yc):
        pc = y_packed(yc)
        for f in range(5):
            hx = x_halo(xc, f)
            for z in range(2):
                t = 2 * f + z
                v = tile(cp, f, z)
                vx[t, 0:8, :] = v
                vx[t, 8:16, :] = hx[z]
                vy[t, :, 0:128] = v
                vy[t, :, 128:256] = y_halo(pc, f, z)

    def grads_of(t):
        return line_grads(fxp[t], fxm[t], 0), line_grads(fyp[t], fym[t], 1)

    def keep_grads(t, _):
        along_x, along_y = grads_of(t)
        for side in range(2):
            for k in range(4):
                kx[t, side, k] = along_x[side][k]
                ky[t, side, k] = along_y[side][k]
        return 0

    def kept_grads(t):
        return (
            [[kx[t, side, k] for k in range(4)] for side in range(2)],
            [[ky[t, side, k] for k in range(4)] for side in range(2)],
        )

    def flux_back(qp, grads_at, speed, after):
        speed8 = jnp.broadcast_to(speed, (8, 128))

        def body(t, _):
            along_x, along_y = grads_at(t)
            total, apart, laplace = line_adjoint(along_x, vx[t], 0, lambda x: x[0:8, :])
            gx_s[t] = 0.5 * total
            total_y, apart_y, laplace_y = line_adjoint(along_y, vy[t], 1, lambda x: x[:, 0:128])
            gy_s[t] = 0.5 * total_y
            viscous = jnp.where(t < 2, 0.0, VISCOSITY).astype(F32)
            gq_s[t] = 0.5 * speed8 * (apart + apart_y) + viscous * (laplace + laplace_y)
            return 0

        lax.fori_loop(0, 10, body, 0, unroll=5)

        for z in range(2):
            q = [tile(qp, f, z) for f in range(5)]
            inv = inverse(q[0])
            vel = [None] + [q[j] * inv for j in (1, 2, 3)]
            square = vel[1] * vel[1] + vel[2] * vel[2] + vel[3] * vel[3]
            pressure = (GAMMA - 1.0) * (q[4] - 0.5 * q[0] * square)
            out = [gq_s[2 * f + z] for f in range(5)]
            for k, store in ((0, gx_s), (1, gy_s)):
                g = [store[2 * f + z] for f in range(5)]
                u = vel[k + 1]
                dp = (GAMMA - 1.0) * (g[k + 1] + g[4] * u)
                du = (g[1] * q[1] + g[2] * q[2] + g[3] * q[3] + g[4] * (q[4] + pressure)) * inv
                out[0] = out[0] - du * u + 0.5 * dp * square
                for j in (1, 2, 3):
                    out[j] = out[j] + g[j] * u - dp * vel[j]
                out[k + 1] = out[k + 1] + g[0] + du
                out[4] = out[4] + g[4] * u + dp
            for f in range(5):
                after(f, z, out[f] + tile(cqp, f, z))

    grads_one = closure_back(q1p, ctp)

    for s in range(len(stages)):
        speeds = end_stage(spd, s, spd_copies, jnp.maximum)
        if s + 1 < len(stages):
            spd_copies = begin_stage(spd, gsend, grecv, s + 1, speeds)
    for c in a_copies:
        c.wait_recv()

    def keep_middle(f, z, value):
        base = f * 16 + z * 8
        gmp[base : base + 8, :] = 0.25 * tile(ctp, f, z) + 0.25 * TIME_STEP * value

    flux_parts_of(q1p, 0, 0, speeds[:, 128:256])
    fill_v(ctp, 5, 1)
    flux_back(q1p, grads_of, speeds[:, 128:256], keep_middle)
    pack(gmp, 15, 3)
    start(c_copies)

    grads_zero = closure_back(q0p, gmp)
    cells = 2 * 8 * 128 * GX * GY * AF
    params = (0.25 * TIME_STEP * grads_one + TIME_STEP * grads_zero) * (1.0 / cells)
    prm_copies = begin_stage(prm, psend, precv, 0, params)

    for c in b_copies:
        c.wait_recv()
    flux_parts_of(q0p, 10, 2, speeds[:, 0:128])
    lax.fori_loop(0, 10, keep_grads, 0)
    for c in c_copies:
        c.wait_recv()
    fill_v(gmp, 15, 3)

    def keep_state(f, z, value):
        base = f * 16 + z * 8
        out_ref[base : base + 8, :] = (
            0.75 * tile(ctp, f, z) + tile(gmp, f, z) + TIME_STEP * value
        )

    flux_back(q0p, kept_grads, speeds[:, 0:128], keep_state)

    for s in range(len(stages)):
        params = end_stage(prm, s, prm_copies, jnp.add)
        if s + 1 < len(stages):
            prm_copies = begin_stage(prm, psend, precv, s + 1, params)
    out_ref[80:88, :] = params

    for c in started:
        c.wait_send()


def spread(packed_ref, out_ref, gwin_ref, gbin_ref, gwout_ref, gbout_ref, sem):
    whole = pltpu.make_async_copy(packed_ref.at[0:80], out_ref, sem)
    whole.start()
    params = packed_ref[80:88, :]
    gwin_ref[...] = params[0:5, 0:64]
    gbin_ref[...] = params[5:6, 0:64]
    gbout_ref[...] = params[6:7, 0:5]
    gwout_ref[...] = pltpu.roll(params, 64, 1)[0:5, 0:64]
    whole.wait()


def solution(mesh):
    sizes = (mesh.shape["gx"], mesh.shape["gy"], mesh.shape["af"])
    group = sum(sizes) if sizes[0] * sizes[1] * sizes[2] > 16 else sizes[0] * sizes[1] * sizes[2]

    def shards(s0, s1, ct, win, b_in, wout, b_out):
        shape = s0.shape
        vmem = pl.BlockSpec(memory_space=pltpu.VMEM)
        big = pltpu.VMEM((128, 128), F32)
        dma = pltpu.SemaphoreType.DMA
        hbm = pl.BlockSpec(memory_space=pltpu.MemorySpace.HBM)
        packed = pl.pallas_call(
            functools.partial(kernel, sizes),
            out_shape=jax.ShapeDtypeStruct((88, 128), F32),
            in_specs=[hbm] * 7,
            out_specs=vmem,
            scratch_shapes=[
                pltpu.VMEM((5, 64), F32), pltpu.VMEM((1, 64), F32),
                pltpu.VMEM((5, 64), F32), pltpu.VMEM((1, 5), F32), dma((7,)),
                big, big, big, big, big, big,
                pltpu.VMEM((64, 32), BF16),
                pltpu.VMEM((64, 32), BF16),
                pltpu.VMEM((16, 256), BF16),
                pltpu.VMEM((8, 128), F32),
                pltpu.VMEM((10, 16, 128), F32),
                pltpu.VMEM((10, 16, 128), F32),
                pltpu.VMEM((10, 8, 256), F32),
                pltpu.VMEM((10, 8, 256), F32),
                pltpu.VMEM((10, 2, 4, 16, 128), F32),
                pltpu.VMEM((10, 2, 4, 8, 256), F32),
                pltpu.VMEM((10, 16, 128), F32),
                pltpu.VMEM((10, 8, 256), F32),
                pltpu.VMEM((10, 8, 128), F32),
                pltpu.VMEM((10, 8, 128), F32),
                pltpu.VMEM((10, 8, 128), F32),
                pltpu.VMEM((2, 20, 8, 128), F32),
                pltpu.VMEM((2, 20, 8, 128), F32),
                pltpu.VMEM((4, 8, 128), F32),
                pltpu.VMEM((2, 4, 8, 128), F32),
                pltpu.VMEM((group, 1, 256), F32),
                pltpu.VMEM((group, 8, 128), F32),
                dma((2, 3)), dma((2, 3)), dma((2, 3)), dma((2, 3)),
                dma((group,)), dma((group,)), dma((group,)), dma((group,)),
            ],
            compiler_params=pltpu.CompilerParams(
                collective_id=0, has_side_effects=True, vmem_limit_bytes=64 * 1024 * 1024
            ),
            name="adjoint",
        )(
            s0.reshape(80, 128), s1.reshape(80, 128), ct.reshape(80, 128),
            win.T, b_in.reshape(1, 64), wout, b_out.reshape(1, 5),
        )
        out, gwin, gbin, gwout, gbout = pl.pallas_call(
            spread,
            out_shape=(
                jax.ShapeDtypeStruct((80, 128), F32),
                jax.ShapeDtypeStruct((5, 64), F32),
                jax.ShapeDtypeStruct((1, 64), F32),
                jax.ShapeDtypeStruct((5, 64), F32),
                jax.ShapeDtypeStruct((1, 5), F32),
            ),
            in_specs=[vmem],
            out_specs=(hbm, vmem, vmem, vmem, vmem),
            scratch_shapes=[dma(())],
            name="spread",
        )(packed)
        return out.reshape(shape), gwin.T, gbin.reshape(64), gwout, gbout.reshape(5)

    field = P(None, "af", ("cases", "gx"), "gy")
    return jax.shard_map(
        shards,
        mesh=mesh,
        in_specs=(field, field, field, P(), P(), P(), P()),
        out_specs=(field, P("cases", None), P("cases"), P("cases", None), P("cases")),
        check_vma=False,
    )
```

```python
import functools

import jax
import jax.numpy as jnp
from jax import lax
from jax.experimental import pallas as pl
from jax.experimental.pallas import tpu as pltpu
from jax.sharding import PartitionSpec as P

MESH = pl.DeviceIdType.MESH
GAMMA = 1.4
TIME_STEP = 0.1
VISCOSITY = 0.2
WENO_EPS = 1e-06
F32 = jnp.float32
BF16 = jnp.bfloat16


def shifted(x, by, axis):
    return pltpu.roll(x, (-by) % x.shape[axis], axis)


def high_low(x):
    high = x.astype(BF16).astype(F32)
    return high, x - high


def inverse(x):
    return pl.reciprocal(x, approx=True)


def weno_grads(d0, d1, d2, d3):
    a0 = 8.0 * d0 - 11.0 * d1
    a1 = 20.0 * d1 - 11.0 * d0
    b0 = 8.0 * d1 - 5.0 * d2
    b1 = 8.0 * d2 - 5.0 * d1
    c0 = 20.0 * d2 - 11.0 * d3
    c1 = 8.0 * d3 - 11.0 * d2
    eps = 6.0 * WENO_EPS
    ra = inverse(eps + (d0 * a0 + d1 * a1))
    rb = inverse(eps + (d1 * b0 + d2 * b1))
    rc = inverse(eps + (d2 * c0 + d3 * c1))
    wa = ra * ra
    wb = 6.0 * (rb * rb)
    wc = 3.0 * (rc * rc)
    ga = 5.0 * d1 - 2.0 * d0
    gb = d1 + 2.0 * d2
    gc = 4.0 * d2 - d3
    inv = inverse(wa + wb + wc)
    mean = (wa * ga + wb * gb + wc * gc) * inv
    ka = wa * inv
    kb = wb * inv
    kc = wc * inv
    ma = 4.0 * ka * ra * (mean - ga)
    mb = 4.0 * kb * rb * (mean - gb)
    mc = 4.0 * kc * rc * (mean - gc)
    return (
        ma * a0 - 2.0 * ka,
        ma * a1 + 5.0 * ka + mb * b0 + kb,
        mb * b1 + 2.0 * kb + mc * c0 + 4.0 * kc,
        mc * c1 - kc,
    )


def line_grads(up, down, axis):
    sh = functools.partial(shifted, axis=axis)
    d = sh(up, 1) - up
    e = down - sh(down, 1)
    return weno_grads(sh(d, -2), sh(d, -1), d, sh(d, 1)), weno_grads(sh(e, 2), sh(e, 1), e, sh(e, -1))


def line_adjoint(grads, v, axis, own):
    sh = functools.partial(shifted, axis=axis)
    ahead = sh(v, 1)
    w = ahead - v
    w6 = w * (1.0 / 6.0)
    wb = sh(w, -1)
    g = [w6 * x for x in grads[0]]
    gp = sh(sh(g[0], 1) + g[1], 1) + g[2] + sh(g[3], -1)
    g = [w6 * x for x in grads[1]]
    gm = sh(sh(g[0], -1) + g[1], -1) + g[2] + sh(g[3], 1)
    t = gp - gm
    s = gp + gm
    total = w + wb + sh(t, -1) - t
    apart = w - wb + sh(s, -1) - s
    return own(total), own(apart), own(w - wb)


def flux_parts(q, k):
    inv = inverse(q[0])
    pressure = (GAMMA - 1.0) * (
        q[4] - 0.5 * (q[1] * q[1] + q[2] * q[2] + q[3] * q[3]) * inv
    )
    u = q[k + 1] * inv
    f = [q[k + 1], q[1] * u, q[2] * u, q[3] * u, (q[4] + pressure) * u]
    f[k + 1] = f[k + 1] + pressure
    return f


def kernel(
    sizes,
    s0_hbm, s1_hbm, ct_hbm, win_hbm, bin_hbm, wout_hbm, bout_hbm,
    out_ref,
    win_ref, bin_ref, wout_ref, bout_ref, in_sem,
    q0p, q1p, ctp, gmp, cqp, wtile, w1, w2, w3, bcol,
    fxp, fxm, fyp, fym, kx, ky, vx, vy, gx_s, gy_s, gq_s,
    xs, xr, ys, yr, spd, prm,
    xsend, xrecv, ysend, yrecv, gsend, grecv, psend, precv,
):
    GX, GY, AF = sizes
    ix, iy, ia = lax.axis_index("gx"), lax.axis_index("gy"), lax.axis_index("af")
    ic = lax.axis_index("cases")
    joint = GX * GY * AF <= 16
    if joint:
        stages = [[(a, b, c) for a in range(GX) for b in range(GY) for c in range(AF)]]
    else:
        stages = [
            [(a, 0, 0) for a in range(GX)],
            [(0, b, 0) for b in range(GY)],
            [(0, 0, c) for c in range(AF)],
        ]

    def place(off):
        return (
            ic,
            lax.rem(ix + off[0], GX) if off[0] else ix,
            lax.rem(iy + off[1], GY) if off[1] else iy,
            lax.rem(ia + off[2], AF) if off[2] else ia,
        )

    loads = []
    for n, (src, dst) in enumerate((
        (s1_hbm, q1p.at[0:80]), (s0_hbm, q0p.at[0:80]), (ct_hbm, ctp.at[0:80]),
        (win_hbm, win_ref), (bin_hbm, bin_ref), (wout_hbm, wout_ref), (bout_hbm, bout_ref),
    )):
        loads.append(pltpu.make_async_copy(src, dst, in_sem.at[n]))
        loads[-1].start()

    barrier = pltpu.get_barrier_semaphore()
    greeted = 0
    for stage in stages:
        for off in stage[1:]:
            pl.semaphore_signal(barrier, inc=1, device_id=place(off), device_id_type=MESH)
            greeted += 1

    row = lax.broadcasted_iota(jnp.int32, (8, 128), 0)
    lane = lax.broadcasted_iota(jnp.int32, (8, 128), 1)
    upper = row < 4

    ones = jnp.ones((16, 128), F32)
    for ref in (q0p, q1p):
        ref[80:96, :] = ones
        ref[96:128, :] = jnp.zeros((32, 128), F32)
    for ref in (ctp, gmp):
        ref[80:128, :] = jnp.zeros((48, 128), F32)

    def tile(ref, f, z):
        return ref[f * 16 + z * 8 : f * 16 + z * 8 + 8, :]

    def pack(ref, base, yslot):
        packed = jnp.zeros((8, 128), F32)
        for f in range(5):
            one, two = tile(ref, f, 0), pltpu.roll(tile(ref, f, 1), 4, 0)
            xs[0, base + f] = jnp.where(upper, one, two)
            xs[1, base + f] = jnp.where(upper, two, one)
            for z in range(2):
                t = f * 2 + z
                moved = pltpu.roll(tile(ref, f, z), (4 + 8 * t) % 128, 1)
                packed = jnp.where((lane >= 8 * t) & (lane < 8 * t + 8), moved, packed)
        ys[yslot] = packed

    def x_copies(base, count, sem):
        made = []
        for way in range(2):
            off = (GX - 1, 0, 0) if way == 0 else (1, 0, 0)
            made.append(
                pltpu.make_async_remote_copy(
                    src_ref=xs.at[way, pl.ds(base, count)],
                    dst_ref=xr.at[way, pl.ds(base, count)],
                    send_sem=xsend.at[way, sem],
                    recv_sem=xrecv.at[way, sem],
                    device_id=place(off),
                    device_id_type=MESH,
                )
            )
        return made

    def y_copies(base, count, sem):
        made = []
        for way in range(1 if GY == 2 else 2):
            off = (0, 1, 0) if way == 0 else (0, GY - 1, 0)
            made.append(
                pltpu.make_async_remote_copy(
                    src_ref=ys.at[pl.ds(base, count)],
                    dst_ref=yr.at[way, pl.ds(base, count)],
                    send_sem=ysend.at[way, sem],
                    recv_sem=yrecv.at[way, sem],
                    device_id=place(off),
                    device_id_type=MESH,
                )
            )
        return made

    def x_halo(base, f):
        ahead, behind = xr[0, base + f], xr[1, base + f]
        return (
            jnp.where(upper, ahead, behind),
            pltpu.roll(jnp.where(upper, behind, ahead), 4, 0),
        )

    def y_packed(slot):
        if GY == 2:
            return yr[0, slot]
        return jnp.where(lax.rem(lane, 8) < 4, yr[0, slot], yr[1, slot])

    def y_halo(packed, f, z):
        return pltpu.roll(packed, (-(4 + 8 * (f * 2 + z))) % 128, 1)


    def top_speed(ref):
        best = None
        for z in range(2):
            q = [tile(ref, f, z) for f in range(5)]
            inv = inverse(q[0])
            pressure = (GAMMA - 1.0) * (
                q[4] - 0.5 * (q[1] * q[1] + q[2] * q[2] + q[3] * q[3]) * inv
            )
            sound = jnp.sqrt(GAMMA * pressure * inv)
            value = jnp.maximum(jnp.abs(q[1] * inv), jnp.abs(q[2] * inv)) + sound
            best = value if best is None else jnp.maximum(best, value)
        best = jnp.max(best, axis=0, keepdims=True)
        return jnp.broadcast_to(jnp.max(best, axis=1, keepdims=True), (1, 128))

    loads[0].wait()
    loads[1].wait()
    fastest = jnp.concatenate([top_speed(q0p), top_speed(q1p)], axis=1)

    loads[2].wait()
    pack(q1p, 0, 0)
    pack(ctp, 5, 1)
    pl.semaphore_wait(barrier, greeted)

    a_copies = x_copies(0, 10, 0) + y_copies(0, 2, 0)
    b_copies = x_copies(10, 5, 1) + y_copies(2, 1, 1)
    c_copies = x_copies(15, 5, 2) + y_copies(3, 1, 2)

    def numbers(stage_index):
        base = sum(len(stages[s]) for s in range(stage_index))
        return [base + k for k in range(len(stages[stage_index]))]

    def my_rank(stage_index):
        if joint:
            return (ix * GY + iy) * AF + ia
        return (ix, iy, ia)[stage_index]

    def group_copies(buf, send, recv, stage_index):
        base = numbers(stage_index)[0]
        rank = base + my_rank(stage_index)
        made = []
        for k, off in enumerate(stages[stage_index]):
            if k == 0:
                continue
            made.append(
                pltpu.make_async_remote_copy(
                    src_ref=buf.at[rank],
                    dst_ref=buf.at[rank],
                    send_sem=send.at[base + k],
                    recv_sem=recv.at[base + k],
                    device_id=place(off),
                    device_id_type=MESH,
                )
            )
        return made

    started = []

    def start(copies):
        for c in copies:
            c.start()
            started.append(c)

    def begin_stage(buf, send, recv, s, value):
        buf[numbers(s)[0] + my_rank(s)] = value
        copies = group_copies(buf, send, recv, s)
        start(copies)
        return copies

    def end_stage(buf, s, copies, op):
        for c in copies:
            c.wait_recv()
        total = None
        for n in numbers(s):
            total = buf[n] if total is None else op(total, buf[n])
        return total

    spd_copies = begin_stage(spd, gsend, grecv, 0, fastest)
    start(a_copies)
    pack(q0p, 10, 2)
    start(b_copies)

    wtile[0:8, :] = jnp.zeros((8, 128), F32)
    for c in loads[3:]:
        c.wait()
    wtile[0:5, 0:64] = win_ref[...]
    wint = wtile[0:8, :]
    wtile[0:5, 0:64] = wout_ref[...]
    wout8 = wtile[0:8, :]
    wtile[0:8, :] = jnp.zeros((8, 128), F32)
    wtile[0:1, 0:64] = bin_ref[...]
    wtile[1:2, 0:5] = bout_ref[...]
    bin_row = wtile[0:1, :]
    bout_row = wtile[1:2, :]
    aug = jnp.where(row == 5, bin_row, wint)
    zero8 = jnp.zeros((8, 128), F32)
    ah, al = high_low(aug)
    oh, ol = high_low(wout8)
    fill = jnp.zeros((96, 128), F32)
    w1[...] = jnp.transpose(jnp.concatenate([ah, ah, al, zero8, fill], axis=0))[0:64, 0:32].astype(BF16)
    w2[...] = jnp.transpose(jnp.concatenate([oh, oh, ol, zero8, fill], axis=0))[0:64, 0:32].astype(BF16)
    ih, il = high_low(wint)
    lo_lane = lane < 64
    first = jnp.where(lo_lane, ih, pltpu.roll(ih, 64, 1))
    w3[:, 0:128] = jnp.concatenate([first, zero8], axis=0).astype(BF16)
    w3[:, 128:256] = jnp.concatenate([jnp.where(lo_lane, il, 0.0), zero8], axis=0).astype(BF16)
    bcol[...] = jnp.broadcast_to(
        jnp.sum(jnp.where(lane == row, jnp.broadcast_to(bout_row, (8, 128)), 0.0), axis=1, keepdims=True),
        (8, 128),
    )


    def closure_back(qp, cp):
        acc = jnp.zeros((32, 256), F32)
        dsum = jnp.zeros((8, 256), F32)
        bb = jnp.concatenate([bcol[...], bcol[...]], axis=1)
        for chunk in range(8):
            r = 2 * chunk
            q8 = jnp.concatenate([qp[pl.ds(r, 8, stride=16), :], qp[pl.ds(r + 1, 8, stride=16), :]], axis=1)
            c8 = jnp.concatenate([cp[pl.ds(r, 8, stride=16), :], cp[pl.ds(r + 1, 8, stride=16), :]], axis=1)
            zero = jnp.zeros((8, 256), F32)
            qh, ql = high_low(q8)
            ch, cl = high_low(c8)
            pre = jnp.dot(w1[...], jnp.concatenate([qh, ql, qh, zero], axis=0).astype(BF16), preferred_element_type=F32)
            g = jnp.dot(w2[...], jnp.concatenate([ch, cl, ch, zero], axis=0).astype(BF16), preferred_element_type=F32)
            h = jnp.tanh(pre)
            t = g * (1.0 - h * h)
            hg = bb * c8
            prod = h * g
            for k in range(8):
                hg = hg + prod[8 * k : 8 * k + 8, :]
            hg = jnp.sum(hg, axis=0, keepdims=True)
            th, tl = high_low(t)
            hh, hl = high_low(h)
            thb, tlb = th.astype(BF16), tl.astype(BF16)
            hhb, hlb = hh.astype(BF16), hl.astype(BF16)
            stack = jnp.concatenate([thb, tlb, thb, jnp.zeros((64, 256), BF16)], axis=0)
            dq = jnp.dot(w3[...], stack, preferred_element_type=F32)[0:8, :]
            dens = q8[0:1, :]
            row2 = lax.broadcasted_iota(jnp.int32, (8, 256), 0)
            dq = dens * dq + jnp.where(row2 == 0, hg, 0.0)
            cqp[pl.ds(r, 8, stride=16), :] = dq[:, 0:128]
            cqp[pl.ds(r + 1, 8, stride=16), :] = dq[:, 128:256]
            pq = dens * q8
            dout = dens * c8
            dsum = dsum + dout
            ph, pw = high_low(pq)
            dh, dl = high_low(dout)
            left = jnp.concatenate([ph, pw, dh, dl], axis=0).astype(BF16)
            right = jnp.concatenate([thb, tlb, hhb, hlb], axis=0)
            acc = acc + lax.dot_general(left, right, (((1,), (1,)), ((), ())), preferred_element_type=F32)
        a = acc[0:8, 0:128]
        a = a + pltpu.roll(a, 64, 1) + acc[8:16, 0:128]
        b = acc[16:24, 128:256]
        b = b + pltpu.roll(b, 64, 1) + acc[24:32, 128:256]
        total = jnp.where(lane < 64, a, pltpu.roll(b, 64, 1))
        d = jnp.sum(dsum[:, 0:128] + dsum[:, 128:256], axis=1, keepdims=True)
        d = jnp.sum(jnp.where(lane == row, d, 0.0), axis=0, keepdims=True)
        return jnp.where(row == 6, d, total)

    def flux_parts_of(qp, xq, yq, speed):
        speed8 = jnp.broadcast_to(speed, (8, 128))
        speed16 = jnp.broadcast_to(speed, (16, 128))
        speed256 = jnp.concatenate([speed8, speed8], axis=1)
        hx = [x_halo(xq, f) for f in range(5)]
        pq = y_packed(yq)
        for z in range(2):
            own = [tile(qp, f, z) for f in range(5)]
            q = [jnp.concatenate([own[f], hx[f][z]], axis=0) for f in range(5)]
            for f, part in enumerate(flux_parts(q, 0)):
                lead = speed16 * q[f]
                fxp[2 * f + z] = 0.5 * (part + lead)
                fxm[2 * f + z] = 0.5 * (part - lead)
            q = [jnp.concatenate([own[f], y_halo(pq, f, z)], axis=1) for f in range(5)]
            for f, part in enumerate(flux_parts(q, 1)):
                lead = speed256 * q[f]
                fyp[2 * f + z] = 0.5 * (part + lead)
                fym[2 * f + z] = 0.5 * (part - lead)

    def fill_v(cp, xc, yc):
        pc = y_packed(yc)
        for f in range(5):
            hx = x_halo(xc, f)
            for z in range(2):
                t = 2 * f + z
                v = tile(cp, f, z)
                vx[t, 0:8, :] = v
                vx[t, 8:16, :] = hx[z]
                vy[t, :, 0:128] = v
                vy[t, :, 128:256] = y_halo(pc, f, z)

    def grads_of(t):
        return line_grads(fxp[t], fxm[t], 0), line_grads(fyp[t], fym[t], 1)

    def keep_grads(t, _):
        along_x, along_y = grads_of(t)
        for side in range(2):
            for k in range(4):
                kx[t, side, k] = along_x[side][k]
                ky[t, side, k] = along_y[side][k]
        return 0

    def kept_grads(t):
        return (
            [[kx[t, side, k] for k in range(4)] for side in range(2)],
            [[ky[t, side, k] for k in range(4)] for side in range(2)],
        )

    def flux_back(qp, grads_at, speed, after):
        speed8 = jnp.broadcast_to(speed, (8, 128))

        def body(t, _):
            along_x, along_y = grads_at(t)
            total, apart, laplace = line_adjoint(along_x, vx[t], 0, lambda x: x[0:8, :])
            gx_s[t] = 0.5 * total
            total_y, apart_y, laplace_y = line_adjoint(along_y, vy[t], 1, lambda x: x[:, 0:128])
            gy_s[t] = 0.5 * total_y
            viscous = jnp.where(t < 2, 0.0, VISCOSITY).astype(F32)
            gq_s[t] = 0.5 * speed8 * (apart + apart_y) + viscous * (laplace + laplace_y)
            return 0

        lax.fori_loop(0, 10, body, 0, unroll=5)

        for z in range(2):
            q = [tile(qp, f, z) for f in range(5)]
            inv = inverse(q[0])
            vel = [None] + [q[j] * inv for j in (1, 2, 3)]
            square = vel[1] * vel[1] + vel[2] * vel[2] + vel[3] * vel[3]
            pressure = (GAMMA - 1.0) * (q[4] - 0.5 * q[0] * square)
            out = [gq_s[2 * f + z] for f in range(5)]
            for k, store in ((0, gx_s), (1, gy_s)):
                g = [store[2 * f + z] for f in range(5)]
                u = vel[k + 1]
                dp = (GAMMA - 1.0) * (g[k + 1] + g[4] * u)
                du = (g[1] * q[1] + g[2] * q[2] + g[3] * q[3] + g[4] * (q[4] + pressure)) * inv
                out[0] = out[0] - du * u + 0.5 * dp * square
                for j in (1, 2, 3):
                    out[j] = out[j] + g[j] * u - dp * vel[j]
                out[k + 1] = out[k + 1] + g[0] + du
                out[4] = out[4] + g[4] * u + dp
            for f in range(5):
                after(f, z, out[f] + tile(cqp, f, z))

    grads_one = closure_back(q1p, ctp)

    for s in range(len(stages)):
        speeds = end_stage(spd, s, spd_copies, jnp.maximum)
        if s + 1 < len(stages):
            spd_copies = begin_stage(spd, gsend, grecv, s + 1, speeds)
    for c in a_copies:
        c.wait_recv()

    def keep_middle(f, z, value):
        base = f * 16 + z * 8
        gmp[base : base + 8, :] = 0.25 * tile(ctp, f, z) + 0.25 * TIME_STEP * value

    flux_parts_of(q1p, 0, 0, speeds[:, 128:256])
    fill_v(ctp, 5, 1)
    flux_back(q1p, grads_of, speeds[:, 128:256], keep_middle)
    pack(gmp, 15, 3)
    start(c_copies)

    grads_zero = closure_back(q0p, gmp)
    cells = 2 * 8 * 128 * GX * GY * AF
    params = (0.25 * TIME_STEP * grads_one + TIME_STEP * grads_zero) * (1.0 / cells)
    prm_copies = begin_stage(prm, psend, precv, 0, params)

    for c in b_copies:
        c.wait_recv()
    flux_parts_of(q0p, 10, 2, speeds[:, 0:128])
    lax.fori_loop(0, 10, keep_grads, 0)
    for c in c_copies:
        c.wait_recv()
    fill_v(gmp, 15, 3)

    def keep_state(f, z, value):
        base = f * 16 + z * 8
        out_ref[base : base + 8, :] = (
            0.75 * tile(ctp, f, z) + tile(gmp, f, z) + TIME_STEP * value
        )

    flux_back(q0p, kept_grads, speeds[:, 0:128], keep_state)

    for s in range(len(stages)):
        params = end_stage(prm, s, prm_copies, jnp.add)
        if s + 1 < len(stages):
            prm_copies = begin_stage(prm, psend, precv, s + 1, params)
    out_ref[80:88, :] = params

    for c in started:
        c.wait_send()


def spread(packed_ref, out_ref, gwin_ref, gbin_ref, gwout_ref, gbout_ref, sem):
    whole = pltpu.make_async_copy(packed_ref.at[0:80], out_ref, sem)
    whole.start()
    params = packed_ref[80:88, :]
    gwin_ref[...] = params[0:5, 0:64]
    gbin_ref[...] = params[5:6, 0:64]
    gbout_ref[...] = params[6:7, 0:5]
    gwout_ref[...] = pltpu.roll(params, 64, 1)[0:5, 0:64]
    whole.wait()


def solution(mesh):
    sizes = (mesh.shape["gx"], mesh.shape["gy"], mesh.shape["af"])
    group = sum(sizes) if sizes[0] * sizes[1] * sizes[2] > 16 else sizes[0] * sizes[1] * sizes[2]

    def shards(s0, s1, ct, win, b_in, wout, b_out):
        shape = s0.shape
        vmem = pl.BlockSpec(memory_space=pltpu.VMEM)
        big = pltpu.VMEM((128, 128), F32)
        dma = pltpu.SemaphoreType.DMA
        hbm = pl.BlockSpec(memory_space=pltpu.MemorySpace.HBM)
        packed = pl.pallas_call(
            functools.partial(kernel, sizes),
            out_shape=jax.ShapeDtypeStruct((88, 128), F32),
            in_specs=[hbm] * 7,
            out_specs=vmem,
            scratch_shapes=[
                pltpu.VMEM((5, 64), F32), pltpu.VMEM((1, 64), F32),
                pltpu.VMEM((5, 64), F32), pltpu.VMEM((1, 5), F32), dma((7,)),
                big, big, big, big, big, big,
                pltpu.VMEM((64, 32), BF16),
                pltpu.VMEM((64, 32), BF16),
                pltpu.VMEM((16, 256), BF16),
                pltpu.VMEM((8, 128), F32),
                pltpu.VMEM((10, 16, 128), F32),
                pltpu.VMEM((10, 16, 128), F32),
                pltpu.VMEM((10, 8, 256), F32),
                pltpu.VMEM((10, 8, 256), F32),
                pltpu.VMEM((10, 2, 4, 16, 128), F32),
                pltpu.VMEM((10, 2, 4, 8, 256), F32),
                pltpu.VMEM((10, 16, 128), F32),
                pltpu.VMEM((10, 8, 256), F32),
                pltpu.VMEM((10, 8, 128), F32),
                pltpu.VMEM((10, 8, 128), F32),
                pltpu.VMEM((10, 8, 128), F32),
                pltpu.VMEM((2, 20, 8, 128), F32),
                pltpu.VMEM((2, 20, 8, 128), F32),
                pltpu.VMEM((4, 8, 128), F32),
                pltpu.VMEM((2, 4, 8, 128), F32),
                pltpu.VMEM((group, 1, 256), F32),
                pltpu.VMEM((group, 8, 128), F32),
                dma((2, 3)), dma((2, 3)), dma((2, 3)), dma((2, 3)),
                dma((group,)), dma((group,)), dma((group,)), dma((group,)),
            ],
            compiler_params=pltpu.CompilerParams(
                collective_id=0, has_side_effects=True, vmem_limit_bytes=64 * 1024 * 1024
            ),
            name="adjoint",
        )(
            s0.reshape(80, 128), s1.reshape(80, 128), ct.reshape(80, 128),
            win.T, b_in.reshape(1, 64), wout, b_out.reshape(1, 5),
        )
        out, gwin, gbin, gwout, gbout = pl.pallas_call(
            spread,
            out_shape=(
                jax.ShapeDtypeStruct((80, 128), F32),
                jax.ShapeDtypeStruct((5, 64), F32),
                jax.ShapeDtypeStruct((1, 64), F32),
                jax.ShapeDtypeStruct((5, 64), F32),
                jax.ShapeDtypeStruct((1, 5), F32),
            ),
            in_specs=[vmem],
            out_specs=(hbm, vmem, vmem, vmem, vmem),
            scratch_shapes=[dma(())],
            name="spread",
        )(packed)
        return out.reshape(shape), gwin.T, gbin.reshape(64), gwout, gbout.reshape(5)

    field = P(None, "af", ("cases", "gx"), "gy")
    return jax.shard_map(
        shards,
        mesh=mesh,
        in_specs=(field, field, field, P(), P(), P(), P()),
        out_specs=(field, P("cases", None), P("cases"), P("cases", None), P("cases")),
        check_vma=False,
    )
```
